32 devices in a mesh: expert: 8 (over z, y), tensor: 4 (over x, core).
Axes of the slice: x: 2, y: 2, z: 4, core: 2. Of those that a mesh axis runs over, the one named last changes fastest.
Arguments:
- tokens: bfloat16 [1024, 8192], P('expert', 'tensor'), may hold values from -25 to 25, as said below
- routes: int32 [1024, 2], P('expert'), may hold values from 0 to 7, all different within a row; in each aligned block of 128 rows (0 to 127, 128 to 255, ...) at most 48 rows name the same one
- norm_gain: float32 [2, 8192], P(None, 'tensor'), may hold values from 0.5 to 1.5
- router_weight: bfloat16 [2, 8192, 8], P(None, 'tensor'), may hold values from -0.0625 to 0.0625
- gate_codes: int32 [2, 8, 4096, 1024], P(None, 'expert', None, 'tensor'), may hold values from 0 to 255
- gate_scales: int32 [2, 8, 64, 1024], P(None, 'expert', None, 'tensor'), may hold values from 8 to 10
- up_codes: int32 [2, 8, 4096, 1024], P(None, 'expert', None, 'tensor'), may hold values from 0 to 255
- up_scales: int32 [2, 8, 64, 1024], P(None, 'expert', None, 'tensor'), may hold values from 8 to 10
- down_codes: int32 [2, 8, 512, 8192], P(None, 'expert', 'tensor'), may hold values from 0 to 255
- down_scales: int32 [2, 8, 8, 8192], P(None, 'expert', 'tensor'), may hold values from 6 to 8
Outputs:
- hidden_out: bfloat16 [1024, 8192], P('expert', 'tensor')
The draws below stay inside these ranges and needn't reach their ends.
Inputs may be any that keep to these rules, and one draw needn't show every extreme that they name: `routes`: in the rows of one index of expert (128 aligned rows) no expert is named by more than 48 rows, a bound that some block reaches; the two experts of a row differ. `tokens`: token activations.
All inputs are finite; a program needn't handle non-finite values.
Results may differ from the reference program's by a relative error of at most 0.029.
Values may be sent and summed in bfloat16 or wider, within the bound.
No kernel may reach another device: no remote copies, remote signals or barrier semaphores. Data moves between devices by JAX's collectives and lax.ppermute only.
A program may use at most 192 MiB of HBM per device.

```python
import math
import jax
import jax.numpy as jnp
import numpy as np
from jax import lax

D = 8192
FF = 1024
GROUP = 128
IN_SHIFT = 9
OUT_SHIFT = 7
LAYERS = 2
TOK_DEV = 128
TOKENS = 1024
EXPERTS = 8
CAP = 48
N_TENSOR = 4


def draw_tokens(key, part):
    columns = jnp.arange(D, dtype=jnp.float32)
    column_ramp = jnp.exp(0.6 * (2.0 * columns / (D - 1) - 1.0))
    values = jnp.clip(jax.random.normal(key, (TOKENS, D), jnp.float32), -6.0, 6.0)
    return (values * column_ramp[None, :]).astype(jnp.bfloat16)


def plant(result, rng, low, top_value):
    shape = result.shape
    index_at = [jax.random.randint(jax.random.fold_in(rng, axis), (), 0, shape[axis]) for axis in range(len(shape))]
    result = result.at[tuple(index_at)].set(low)
    longest = shape.index(max(shape))
    index_at[longest] = (index_at[longest] + 1) % shape[longest]
    return result.at[tuple(index_at)].set(top_value)


def levels(rng, dims, shards, smallest, top_value):
    loudness, own = 1.0, jax.random.fold_in(rng, 6)
    for position, parts in shards:
        steps = jnp.exp(jax.random.uniform(jax.random.fold_in(own, position), (parts,), jnp.float32, smallest / len(shards), top_value / len(shards)))
        loudness = loudness * jnp.repeat(steps, dims[position] // parts).reshape([-1 if axis == position else 1 for axis in range(len(dims))])
    return loudness


def shared_out(rng, own, number, rows, number_of, top, bound, skew):
    ranking = jax.random.permutation(rng, number_of)
    heavy_load, usual = shares(number_of, rows * top, bound, skew, True), shares(number_of, rows * top, bound, skew, False)
    places = jnp.arange(number_of)

    def named(sizes, rotation):
        used = int((sizes > 0).sum())
        fixed = max(1, used // 4)
        shifted = fixed + (places - fixed + rotation * (used - fixed)) % max(1, number_of - fixed)
        return jnp.zeros((number_of,), jnp.int32).at[ranking[jnp.where(places < fixed, places, shifted)]].set(jnp.asarray(sizes, jnp.int32))

    sizes = jnp.where(number % 4 == 0, named(heavy_load, number // 4), named(usual, number - number // 4 - 1))
    mixed = jax.random.permutation(jax.random.fold_in(own, 3), number_of)
    source_of, taker = mixed[0:number_of // 2 * 2:2], mixed[1:number_of // 2 * 2:2]
    margin = jnp.minimum(sizes[source_of] - 1, bound - sizes[taker]) // 2
    margin = jnp.where((source_of == ranking[0]) | (taker == ranking[0]) | (sizes[taker] == 0), 0, jnp.maximum(margin, 0))
    shifted = jax.random.randint(jax.random.fold_in(own, 4), (number_of // 2,), 0, 1 << 20) % (margin + 1)
    sizes = sizes.at[source_of].add(-shifted).at[taker].add(shifted)
    members = jnp.searchsorted(jnp.cumsum(sizes), jnp.arange(rows * top), side="right").astype(jnp.int32)
    grid = members.reshape(top, rows).T
    grid = grid[jax.random.permutation(jax.random.fold_in(own, 1), rows)]
    rotation = jax.random.randint(jax.random.fold_in(own, 2), (rows, 1), 0, top)
    return jnp.take_along_axis(grid, (jnp.arange(top)[None, :] + rotation) % top, axis=1)


def shares(amount, total, limit, slope, full):
    weights = [(1 << 20) // math.isqrt(grade ** slope) + 1 for grade in range(1, amount + 1)]
    largest = limit if full else min(limit, max(-(-total // amount), total * weights[0] // sum(weights)))
    least = 1 if total - largest >= amount - 1 else 0
    holding, surplus = [largest] + [least] * (amount - 1), total - largest - least * (amount - 1)
    while surplus > 0:
        free = [i for i in range(1, amount) if holding[i] < largest] or [i for i in range(1, amount) if holding[i] < limit]
        mass, budget = sum([weights[i] for i in free]), surplus
        for i in free:
            addition = min(limit - holding[i], max(1, budget * weights[i] // mass), surplus)
            holding[i] = holding[i] + addition
            surplus = surplus - addition
    return np.array(holding)


def normal_values(own_key, dims, deviation, bound, pieces=(), kind=jnp.bfloat16):
    values = jax.random.normal(own_key, dims, jnp.float32) * deviation
    if len(pieces) > 0:
        values = levels(own_key, dims, pieces, -0.22, 0.18) * values
    return jnp.clip(values, min=-bound, max=bound).astype(kind)


def setup_inputs(seed: int = 0) -> dict:
    key_of = jax.random.split(jax.random.key(seed), 11)
    tokens = draw_tokens(jax.random.fold_in(key_of[10], 71), 0)
    routes_keys = jax.random.split(jax.random.fold_in(key_of[1], 1), TOKENS // TOK_DEV)
    routes_turns = jax.random.permutation(jax.random.fold_in(key_of[1], 3), TOKENS // TOK_DEV)
    routes = jax.vmap(lambda own, number: shared_out(jax.random.fold_in(key_of[1], 2), own, number, TOK_DEV, EXPERTS, 2, CAP, 2))(routes_keys, routes_turns).reshape((TOKENS, 2))
    norm_gain = jnp.clip(1.0 + 0.1 * jax.random.normal(key_of[2], (LAYERS, D), jnp.float32), 0.5, 1.5)
    router_weight = normal_values(key_of[3], (LAYERS, D, EXPERTS), D ** -0.5, 0.0625, ((1, 4),))
    gate_codes = plant(jax.random.randint(key_of[4], (LAYERS, EXPERTS, D // 2, FF), 0, 256), jax.random.fold_in(key_of[4], 1), 0, 255).astype(jnp.int32)
    gate_scales = plant(jax.random.randint(key_of[5], (LAYERS, EXPERTS, D // GROUP, FF), IN_SHIFT - 1, IN_SHIFT + 2), jax.random.fold_in(key_of[5], 1), IN_SHIFT - 1, (IN_SHIFT + 2) - 1).astype(jnp.int32)
    up_codes = plant(jax.random.randint(key_of[6], (LAYERS, EXPERTS, D // 2, FF), 0, 256), jax.random.fold_in(key_of[6], 1), 0, 255).astype(jnp.int32)
    up_scales = plant(jax.random.randint(key_of[7], (LAYERS, EXPERTS, D // GROUP, FF), IN_SHIFT - 1, IN_SHIFT + 2), jax.random.fold_in(key_of[7], 1), IN_SHIFT - 1, (IN_SHIFT + 2) - 1).astype(jnp.int32)
    down_codes = plant(jax.random.randint(key_of[8], (LAYERS, EXPERTS, FF // 2, D), 0, 256), jax.random.fold_in(key_of[8], 1), 0, 255).astype(jnp.int32)
    down_scales = plant(jax.random.randint(key_of[9], (LAYERS, EXPERTS, FF // GROUP, D), OUT_SHIFT - 1, OUT_SHIFT + 2), jax.random.fold_in(key_of[9], 1), OUT_SHIFT - 1, (OUT_SHIFT + 2) - 1).astype(jnp.int32)
    return {"tokens": tokens, "routes": routes, "norm_gain": norm_gain, "router_weight": router_weight, "gate_codes": gate_codes, "gate_scales": gate_scales, "up_codes": up_codes, "up_scales": up_scales, "down_codes": down_codes, "down_scales": down_scales}


def hadamard(table_order):
    matrix = np.ones((1, 1), np.float32)
    for repeat_idx in range(table_order.bit_length() - 1):
        matrix = np.kron(np.array([[1.0, 1.0], [1.0, -1.0]], np.float32), matrix)
    return matrix

def unpack(words):
    shifts = (jnp.arange(2, dtype=jnp.int32) * 4).astype(jnp.int32)
    nibbles = jnp.bitwise_and(jnp.right_shift(words[:, None, :], shifts[None, :, None]), 15) - 8
    return nibbles.reshape(words.shape[0] * 2, words.shape[1]).astype(jnp.int32)

def dequant(words, scales):
    codes = unpack(words)
    groups = scales.shape[0]
    shaped = codes.reshape(groups, codes.shape[0] // groups, codes.shape[1]).astype(jnp.float32)
    factor = jnp.exp2(-scales.astype(jnp.float32))
    return (shaped * factor[:, None, :]).reshape(codes.shape).astype(jnp.bfloat16)

def rotate_rows(matrix_rows):
    row_count = matrix_rows.shape[0]
    local_width = D // N_TENSOR
    first_order = 1 << (local_width.bit_length() - 1) // 2
    second_order = local_width // first_order
    first_table = jnp.asarray(hadamard(first_order), jnp.float32)
    second_table = jnp.asarray(hadamard(second_order), jnp.float32)
    cross_table = jnp.asarray(hadamard(N_TENSOR), jnp.float32)
    blocks = matrix_rows.reshape(row_count, N_TENSOR, first_order, second_order).astype(jnp.float32)
    section_one = jnp.einsum('rnab,bc->rnac', blocks, second_table, precision=lax.Precision.HIGHEST)
    section_two = jnp.einsum('rnac,ad->rndc', section_one, first_table, precision=lax.Precision.HIGHEST)
    section_two = section_two.reshape(row_count, N_TENSOR, local_width)
    outer_sum = jnp.einsum('rne,nm->rme', section_two, cross_table, precision=lax.Precision.HIGHEST)
    return (outer_sum.reshape(row_count, D) * (1.0 / math.sqrt(D))).astype(jnp.bfloat16)

def reference(tokens, routes, norm_gain, router_weight, gate_codes, gate_scales, up_codes, up_scales, down_codes, down_scales):
    block_count = TOKENS // TOK_DEV
    flat_routes = routes.reshape(block_count, 2 * TOK_DEV)
    onehot = (flat_routes[:, :, None] == jnp.arange(EXPERTS, dtype=jnp.int32)[None, None, :]).astype(jnp.int32)
    earlier = jnp.cumsum(onehot, axis=1) - onehot
    ranks = lax.optimization_barrier(jnp.sum(earlier * onehot, axis=2))
    positions = (jnp.arange(block_count, dtype=jnp.int32)[:, None] * CAP + ranks).astype(jnp.int32)
    positions = positions.reshape(TOKENS, 2)
    token_ids = (jnp.arange(2 * TOKENS, dtype=jnp.int32) // 2).astype(jnp.int32)
    owner_table = jnp.full((EXPERTS, block_count * CAP), -1, jnp.int32)
    owner_table = owner_table.at[routes.reshape(-1), positions.reshape(-1)].set(token_ids)
    local_hidden = FF // N_TENSOR
    stream = tokens.astype(jnp.float32)
    for layer_idx in range(LAYERS):
        square = lax.optimization_barrier(jnp.sum(stream * stream, axis=1))
        normed = (stream * lax.rsqrt(square / D + 1e-05)[:, None] * norm_gain[layer_idx][None, :]).astype(jnp.bfloat16)
        logits = jnp.dot(normed, router_weight[layer_idx], preferred_element_type=jnp.float32)
        chosen = jnp.take_along_axis(logits, routes, axis=1)
        first_weight = jax.nn.sigmoid(chosen[:, 0] - chosen[:, 1])
        rotated = rotate_rows(normed)

        def run_expert(operands):
            slot_tokens, gate_c, gate_s, up_c, up_s, down_c, down_s = operands
            inputs = jnp.where((slot_tokens >= 0)[:, None], rotated[jnp.maximum(slot_tokens, 0)], jnp.zeros((), jnp.bfloat16))
            gate_out = jnp.dot(inputs, dequant(gate_c, gate_s), preferred_element_type=jnp.float32)
            up_out = jnp.dot(inputs, dequant(up_c, up_s), preferred_element_type=jnp.float32)
            activ = (jax.nn.silu(gate_out) * up_out).astype(jnp.bfloat16)
            slot_count = activ.shape[0]
            down_full = dequant(down_c, down_s).reshape(N_TENSOR, local_hidden, D).astype(jnp.float32)
            partials = jnp.einsum('sna,nad->snd', activ.reshape(slot_count, N_TENSOR, local_hidden).astype(jnp.float32), down_full, precision=lax.Precision.HIGHEST)
            rounded = lax.optimization_barrier(partials.astype(jnp.bfloat16)).astype(jnp.float32)
            return lax.optimization_barrier(jnp.sum(rounded, axis=1)).astype(jnp.bfloat16)
        expert_all = lax.map(run_expert, (owner_table, gate_codes[layer_idx], gate_scales[layer_idx], up_codes[layer_idx], up_scales[layer_idx], down_codes[layer_idx], down_scales[layer_idx]))
        picked = expert_all[routes, positions].astype(jnp.float32)
        stream = stream + first_weight[:, None] * picked[:, 0] + (1.0 - first_weight)[:, None] * picked[:, 1]
    return stream.astype(jnp.bfloat16)
```

```python
import functools
import math

import jax
import jax.numpy as jnp
import numpy as np
from jax import lax
from jax.experimental import pallas as pl
from jax.experimental.pallas import tpu as pltpu
from jax.sharding import PartitionSpec as P

LAYERS = 2
GROUP = 128
BLOCK = 256
MIB = 1 << 20
FIRST = 4
SECOND = 32
NT = (((1,), (1,)), ((), ()))
TN = (((0,), (0,)), ((), ()))


def exchange(shard, axis, mask):
    return lax.ppermute(shard, axis, [(i, i ^ mask) for i in range(lax.axis_size(axis))])


def block_table():
    index = np.arange(BLOCK)
    order = np.concatenate([index[0::2], index[1::2]])
    common = index[:, None] & order[None, :]
    ones = np.array([bin(v).count("1") for v in range(BLOCK)])[common]
    return np.where(ones % 2 == 1, -1.0, 1.0).astype(np.float32)


def split_table(width):
    table = np.zeros((width, width), np.float32)
    for unit in range(width):
        table[unit, unit % 2 * (width // 2) + unit // 2] = 1.0
    return table


def power(exponents):
    return (1 << (16 - exponents)).astype(jnp.float32) * (1.0 / 65536.0)


SHORT = pl.CostEstimate(flops=1000, bytes_accessed=1000, transcendentals=0)


def butterfly(rows, start):
    stride = start
    while stride < len(rows):
        for b in range(len(rows)):
            if b & stride == 0:
                low, high = rows[b], rows[b + stride]
                rows[b], rows[b + stride] = low + high, low - high
        stride *= 2


def in_weights_kernel(first_steps, words_ref, scales_ref, table_ref, out_ref, sums_ref):
    half = BLOCK // 2
    words_group = GROUP // 2
    groups_block = BLOCK // GROUP
    step = pl.program_id(0)
    width = words_ref.shape[3]
    block_count = out_ref.shape[0]

    @pl.when(step < first_steps)
    def _():
        sums = []
        for q in range(FIRST):
            words = words_ref[0, 0, q * half : (q + 1) * half, :]
            pieces = []
            for shift in (0, 4):
                codes = ((words >> shift) & 15).astype(jnp.float32) - 8.0
                for g in range(groups_block):
                    at = q * groups_block + g
                    factor = power(scales_ref[0, 0, at : at + 1, :])
                    pieces.append(codes[g * words_group : (g + 1) * words_group] * factor)
            block = jnp.concatenate(pieces, axis=0).astype(jnp.bfloat16)
            sums.append(jnp.dot(table_ref[...], block, preferred_element_type=jnp.float32))
        butterfly(sums, 1)
        for q in range(FIRST):
            sums_ref[step * FIRST + q] = sums[q]

    @pl.when(step >= first_steps)
    def _():
        base = (step - first_steps) * SECOND
        for r in range(0, SECOND, 16):
            for c in range(0, width, 128):
                for q in range(FIRST):
                    rows = [
                        sums_ref[b * FIRST + q, pl.ds(pl.multiple_of(base + r, 16), 16), c : c + 128]
                        for b in range(block_count // FIRST)
                    ]
                    butterfly(rows, 1)
                    for b, row in enumerate(rows):
                        out_ref[b * FIRST + q, r : r + 16, c : c + 128] = row.astype(jnp.bfloat16)


def in_weights(words, scales, table, layer_idx):
    _, _, word_rows, width = words.shape
    full = 2 * word_rows
    block_count = full // BLOCK
    first_steps = block_count // FIRST
    word_tile = FIRST * BLOCK // 2
    group_tile = FIRST * BLOCK // GROUP
    out = pl.pallas_call(
        functools.partial(in_weights_kernel, first_steps),
        grid=(first_steps + BLOCK // SECOND,),
        in_specs=[
            pl.BlockSpec(
                (1, 1, word_tile, width),
                lambda i: (layer_idx, 0, jnp.minimum(i, first_steps - 1), 0),
            ),
            pl.BlockSpec(
                (1, 1, group_tile, width),
                lambda i: (layer_idx, 0, jnp.minimum(i, first_steps - 1), 0),
            ),
            pl.BlockSpec((BLOCK, BLOCK), lambda i: (0, 0)),
        ],
        out_specs=pl.BlockSpec(
            (block_count, SECOND, width), lambda i: (0, jnp.maximum(i - first_steps, 0), 0)
        ),
        out_shape=jax.ShapeDtypeStruct((block_count, BLOCK, width), jnp.bfloat16),
        scratch_shapes=[pltpu.VMEM((block_count, BLOCK, width), jnp.float32)],
        compiler_params=pltpu.CompilerParams(vmem_limit_bytes=54 * MIB),
        cost_estimate=SHORT,
        name="in_weights",
    )(words, scales, table)
    return out.reshape(full, width)


def out_weights_kernel(words_ref, scales_ref, out_ref):
    words = words_ref[0, 0]
    word_rows = words.shape[0]
    words_group = GROUP // 2
    for part, shift in enumerate((0, 4)):
        codes = ((words >> shift) & 15).astype(jnp.float32) - 8.0
        for g in range(word_rows // words_group):
            factor = power(scales_ref[0, 0, pl.ds(g, 1), :])
            out_ref[pl.ds(part * word_rows + g * words_group, words_group), :] = (
                codes[g * words_group : (g + 1) * words_group] * factor
            ).astype(jnp.bfloat16)


def out_weights(words, scales, layer_idx):
    _, _, word_rows, width = words.shape
    groups = scales.shape[2]
    tile = 1024
    return pl.pallas_call(
        out_weights_kernel,
        grid=(width // tile,),
        in_specs=[
            pl.BlockSpec((1, 1, word_rows, tile), lambda c: (layer_idx, 0, 0, c)),
            pl.BlockSpec((1, 1, groups, tile), lambda c: (layer_idx, 0, 0, c)),
        ],
        out_specs=pl.BlockSpec((2 * word_rows, tile), lambda c: (0, c)),
        out_shape=jax.ShapeDtypeStruct((2 * word_rows, width), jnp.bfloat16),
        compiler_params=pltpu.CompilerParams(vmem_limit_bytes=54 * MIB),
        cost_estimate=SHORT,
        name="out_weights",
    )(words, scales)


def expert_kernel(part_count, full_width, index_ref, *refs):
    x_refs = refs[:part_count]
    gain_ref, gate_ref, up_ref, down_ref, split_ref = refs[part_count : part_count + 5]
    out_refs = refs[part_count + 5 : 2 * part_count + 5]
    gate_acc, up_acc, square_acc, act_ref = refs[2 * part_count + 5 :]
    step = pl.program_id(0)

    for j in range(part_count):

        @pl.when(step == j)
        def _(j=j):
            rows = x_refs[j][...]
            wide = rows.astype(jnp.float32)
            rows = (wide * gain_ref[...]).astype(jnp.bfloat16)
            gate = jnp.dot(rows, gate_ref[...], preferred_element_type=jnp.float32)
            up = jnp.dot(rows, up_ref[...], preferred_element_type=jnp.float32)
            square = jnp.sum(wide * wide, axis=1, keepdims=True)
            if j > 0:
                gate = gate + gate_acc[...]
                up = up + up_acc[...]
                square = square + square_acc[...]
            if j < part_count - 1:
                gate_acc[...] = gate
                up_acc[...] = up
                square_acc[...] = square
            else:
                scale = lax.rsqrt(square / full_width + 1e-05) * (1.0 / math.sqrt(full_width))
                gate = gate * scale
                act = (gate / (1.0 + jnp.exp(-gate))) * (up * scale)
                act_ref[...] = jnp.dot(
                    act.astype(jnp.bfloat16), split_ref[...], preferred_element_type=jnp.float32
                ).astype(jnp.bfloat16)

    for j in range(part_count):

        @pl.when(step == part_count + j)
        def _(j=j):
            out_refs[j][...] = jnp.dot(
                act_ref[...], down_ref[...], preferred_element_type=jnp.float32
            ).astype(jnp.bfloat16)


def expert_parts(index, parts, gain, gate_w, up_w, down_w, split):
    part_count = len(parts)
    row_count, width = parts[0].shape
    full_width, hidden = gate_w.shape
    whole = pl.BlockSpec((row_count, width), lambda i, t: (0, 0))
    last = part_count - 1
    in_block = pl.BlockSpec((width, hidden), lambda i, t: (jnp.minimum(i, last) ^ t[0], 0))
    return pl.pallas_call(
        functools.partial(expert_kernel, part_count, full_width),
        grid_spec=pltpu.PrefetchScalarGridSpec(
            num_scalar_prefetch=1,
            grid=(2 * part_count,),
            in_specs=[whole] * part_count
            + [
                pl.BlockSpec((1, width), lambda i, t: (0, jnp.minimum(i, last) ^ t[0])),
                in_block,
                in_block,
                pl.BlockSpec(
                    (hidden, width), lambda i, t: (0, jnp.maximum(i - part_count, 0) ^ t[0])
                ),
                pl.BlockSpec((hidden, hidden), lambda i, t: (0, 0)),
            ],
            out_specs=[whole] * part_count,
            scratch_shapes=[
                pltpu.VMEM((row_count, hidden), jnp.float32),
                pltpu.VMEM((row_count, hidden), jnp.float32),
                pltpu.VMEM((row_count, 1), jnp.float32),
                pltpu.VMEM((row_count, hidden), jnp.bfloat16),
            ],
        ),
        out_shape=[jax.ShapeDtypeStruct((row_count, width), jnp.bfloat16)] * part_count,
        compiler_params=pltpu.CompilerParams(vmem_limit_bytes=40 * MIB),
        cost_estimate=SHORT,
        name="expert_parts",
    )(index, *parts, gain, gate_w, up_w, down_w, split)


def add_split_kernel(term_count, *refs):
    total = refs[0][...].astype(jnp.float32)
    for term in refs[1:term_count]:
        total = total + term[...].astype(jnp.float32)
    at = 0
    for out in refs[term_count:]:
        rows = out.shape[0]
        out[...] = total[at : at + rows].astype(jnp.bfloat16)
        at += rows


def add_split(terms, piece_rows):
    row_count, width = terms[0].shape
    return pl.pallas_call(
        functools.partial(add_split_kernel, len(terms)),
        out_shape=[
            jax.ShapeDtypeStruct((piece_rows, width), jnp.bfloat16)
            for _ in range(row_count // piece_rows)
        ],
        compiler_params=pltpu.CompilerParams(vmem_limit_bytes=32 * MIB),
        cost_estimate=SHORT,
        name="add_split",
    )(*terms)


def make_stats(stream, gain, router):
    scaled = (stream * gain).astype(jnp.bfloat16)
    logits = lax.dot_general(router, scaled, NT, preferred_element_type=jnp.float32)
    squares = stream * stream
    high = squares.astype(jnp.bfloat16)
    low = (squares - high.astype(jnp.float32)).astype(jnp.bfloat16)
    ones = jnp.ones((8, stream.shape[1]), jnp.bfloat16)
    square = lax.dot_general(ones, high, NT, preferred_element_type=jnp.float32) + lax.dot_general(
        ones, low, NT, preferred_element_type=jnp.float32
    )
    return logits, square


def fill_slots(picks, rows, slot_refs):
    gathered = jnp.dot(picks, rows, preferred_element_type=jnp.float32)
    capacity = slot_refs[0].shape[0]
    for k, out in enumerate(slot_refs):
        out[...] = gathered[k * capacity : (k + 1) * capacity].astype(jnp.bfloat16)


def enter_kernel(expert_count, me_ref, routes_ref, tokens_ref, gain_ref, router_ref, *refs):
    picks_ref, stats_ref = refs[:2]
    slot_refs = refs[2:]
    token_count = tokens_ref.shape[0]
    capacity = slot_refs[0].shape[0]
    relative = lax.broadcasted_iota(jnp.int32, (expert_count, token_count), 0) ^ me_ref[0]
    first, second = routes_ref[0:1, :], routes_ref[1:2, :]
    member = ((relative == first) | (relative == second)).astype(jnp.float32)
    before = lax.broadcasted_iota(jnp.int32, (token_count, token_count), 0)
    after = lax.broadcasted_iota(jnp.int32, (token_count, token_count), 1)
    earlier = (before < after).astype(jnp.bfloat16)
    ranks = jnp.dot(member.astype(jnp.bfloat16), earlier, preferred_element_type=jnp.float32)
    position = lax.broadcasted_iota(jnp.int32, (capacity, token_count), 0).astype(jnp.float32)
    pieces = [
        jnp.where(position == ranks[k : k + 1, :], member[k : k + 1, :], 0.0)
        for k in range(expert_count)
    ]
    picks = jnp.concatenate(pieces, axis=0).astype(jnp.bfloat16)
    picks_ref[...] = picks
    tokens = tokens_ref[...]
    fill_slots(picks, tokens, slot_refs)
    logits, square = make_stats(tokens.astype(jnp.float32), gain_ref[...], router_ref[...])
    stats_ref[0:expert_count, :] = logits
    stats_ref[expert_count:, :] = square


def enter(me, routes, tokens, gain, router, capacity):
    token_count, width = tokens.shape
    expert_count = router.shape[0]
    vmem = pl.BlockSpec(memory_space=pltpu.VMEM)
    return pl.pallas_call(
        functools.partial(enter_kernel, expert_count),
        in_specs=[pl.BlockSpec(memory_space=pltpu.SMEM)] + [vmem] * 4,
        out_shape=[
            jax.ShapeDtypeStruct((expert_count * capacity, token_count), jnp.bfloat16),
            jax.ShapeDtypeStruct((expert_count + 8, token_count), jnp.float32),
        ]
        + [jax.ShapeDtypeStruct((capacity, width), jnp.bfloat16)] * expert_count,
        compiler_params=pltpu.CompilerParams(vmem_limit_bytes=32 * MIB),
        cost_estimate=SHORT,
        name="enter",
    )(me, routes, tokens, gain, router)


def combine_kernel(expert_count, piece_count, full_width, last, me_ref, *refs):
    routes_ref, picks_ref, stats_ref, stream_ref = refs[:4]
    piece_refs = refs[4 : 4 + piece_count]
    rest = refs[4 + piece_count :]
    token_count = stream_ref.shape[0]
    capacity = picks_ref.shape[0] // expert_count
    first, second = routes_ref[0:1, :], routes_ref[1:2, :]
    logits = stats_ref[0:expert_count, :]
    scale = lax.rsqrt(stats_ref[expert_count : expert_count + 1, :] / full_width + 1e-05)
    expert = lax.broadcasted_iota(jnp.int32, (expert_count, token_count), 0)
    first_logit = jnp.sum(jnp.where(expert == first, logits, 0.0), axis=0, keepdims=True)
    second_logit = jnp.sum(jnp.where(expert == second, logits, 0.0), axis=0, keepdims=True)
    first_weight = 1.0 / (1.0 + jnp.exp((second_logit - first_logit) * scale))
    second_weight = 1.0 - first_weight
    relative = expert ^ me_ref[0]
    weight = jnp.where(relative == first, first_weight, 0.0) + jnp.where(
        relative == second, second_weight, 0.0
    )
    picks = picks_ref[...]
    wide_picks = picks.astype(jnp.float32)
    weighted = jnp.concatenate(
        [
            wide_picks[k * capacity : (k + 1) * capacity] * weight[k : k + 1, :]
            for k in range(expert_count)
        ],
        axis=0,
    )
    high = weighted.astype(jnp.bfloat16)
    low = (weighted - high.astype(jnp.float32)).astype(jnp.bfloat16)
    outs = [piece[...] for piece in piece_refs]
    outs = outs[0] if len(outs) == 1 else jnp.concatenate(outs, axis=0)
    added = lax.dot_general(high, outs, TN, preferred_element_type=jnp.float32)
    added = added + lax.dot_general(low, outs, TN, preferred_element_type=jnp.float32)
    stream = stream_ref[...].astype(jnp.float32) + added
    if last:
        rest[0][...] = stream.astype(jnp.bfloat16)
        return
    gain_ref, router_ref, next_ref, next_stats_ref = rest[:4]
    next_ref[...] = stream
    fill_slots(picks, stream.astype(jnp.bfloat16), rest[4:])
    logits, square = make_stats(stream, gain_ref[...], router_ref[...])
    next_stats_ref[0:expert_count, :] = logits
    next_stats_ref[expert_count:, :] = square


def combine(me, routes, picks, stats, stream, pieces, full_width, following):
    token_count, width = stream.shape
    expert_count = stats.shape[0] - 8
    capacity = picks.shape[0] // expert_count
    if capacity % 16:
        pieces = [jnp.concatenate(pieces, axis=0)]
    vmem = pl.BlockSpec(memory_space=pltpu.VMEM)
    operands = [routes, picks, stats, stream, *pieces]
    if following is None:
        out_shape = [jax.ShapeDtypeStruct((token_count, width), jnp.bfloat16)]
    else:
        operands += following
        out_shape = [
            jax.ShapeDtypeStruct((token_count, width), jnp.float32),
            jax.ShapeDtypeStruct(stats.shape, jnp.float32),
        ] + [jax.ShapeDtypeStruct((capacity, width), jnp.bfloat16)] * expert_count
    return pl.pallas_call(
        functools.partial(
            combine_kernel, expert_count, len(pieces), full_width, following is None
        ),
        in_specs=[pl.BlockSpec(memory_space=pltpu.SMEM)] + [vmem] * len(operands),
        out_shape=out_shape,
        compiler_params=pltpu.CompilerParams(vmem_limit_bytes=32 * MIB),
        cost_estimate=SHORT,
        name="combine",
    )(me, *operands)


def ordered(value, *earlier):
    return lax.optimization_barrier((value, earlier))[0]


def gather_parts(parts, bits):
    parts = dict(parts)
    for bit in bits:
        for j in sorted(parts):
            parts[j ^ 1 << bit] = exchange(parts[j], "tensor", 1 << bit)
    return parts


def reduce_parts(terms, bit):
    kept = {j: list(parts) for j, parts in terms.items() if not j >> bit & 1}
    for j, parts in terms.items():
        if j >> bit & 1:
            total = parts[0]
            if len(parts) > 1:
                total = sum(part.astype(jnp.float32) for part in parts).astype(jnp.bfloat16)
            kept[j ^ 1 << bit].append(exchange(total, "tensor", 1 << bit))
    return kept


def settle(terms):
    return {
        j: parts
        if j == 0 or len(parts) == 1
        else [sum(part.astype(jnp.float32) for part in parts).astype(jnp.bfloat16)]
        for j, parts in terms.items()
    }


def per_device(
    tokens,
    routes,
    norm_gain,
    router_weight,
    gate_codes,
    gate_scales,
    up_codes,
    up_scales,
    down_codes,
    down_scales,
):
    part_count = lax.axis_size("tensor")
    expert_count = lax.axis_size("expert")
    bits = part_count.bit_length() - 1
    token_count, width = tokens.shape
    full_width = width * part_count
    hidden = gate_codes.shape[3]
    capacity = 3 * token_count // expert_count
    me = lax.axis_index("expert").astype(jnp.int32).reshape(1)
    index = lax.axis_index("tensor").astype(jnp.int32).reshape(1)
    table = jnp.asarray(block_table(), jnp.bfloat16)
    split = jnp.asarray(split_table(hidden), jnp.bfloat16)
    routes_rows = routes.T
    router_rows = jnp.swapaxes(router_weight, 1, 2)

    picks, stats, *slots = enter(
        me, routes_rows, tokens, norm_gain[0:1], router_rows[0], capacity
    )
    whole_gain = lax.all_gather(norm_gain, "tensor", axis=1, tiled=True)

    quarter = expert_count // 4
    near = list(range(2 * quarter))
    far = [list(range(2 * quarter, 3 * quarter)), list(range(3 * quarter, 4 * quarter))]
    first_bits, core_bits = list(reversed(range(1, bits))), [0]
    stream = tokens

    def stack(pieces, *earlier):
        return jnp.concatenate(ordered(pieces, *earlier), axis=0)

    def gather_first(rows):
        return gather_parts({0: rows}, first_bits)

    def cores_added(outs):
        return settle(reduce_parts({j: [part] for j, part in enumerate(outs)}, 0))

    def rest_added(terms):
        for bit in range(1, bits):
            terms = reduce_parts(terms, bit)
        return terms[0]

    def give_back(terms, chunk, returned):
        pieces = add_split(terms, capacity)
        for k, piece in zip(chunk, pieces):
            returned[k] = piece if k == 0 else exchange(piece, "expert", k)
        return pieces

    weights = None
    for layer_idx in range(LAYERS):
        gain = whole_gain[layer_idx : layer_idx + 1]
        arrived = [slots[0]] + [
            exchange(slots[k], "expert", k) for k in range(1, expert_count)
        ]
        returned = [None] * expert_count
        near_parts = gather_first(stack([arrived[k] for k in near]))
        if weights is None:
            later = ordered(table, near_parts[0])
            gate_w = in_weights(gate_codes, gate_scales, later, layer_idx)
            near_parts = ordered(near_parts, gate_w)
            later = ordered(table, near_parts)
            near_parts = gather_parts(near_parts, core_bits)
            up_w = in_weights(up_codes, up_scales, later, layer_idx)
            down_w = out_weights(down_codes, ordered(down_scales, up_w), layer_idx)
            weights = (gate_w, up_w, down_w)
            far_rows = stack([arrived[k] for k in far[0]], up_w)
        else:
            near_parts = gather_parts(near_parts, core_bits)
            far_rows = stack([arrived[k] for k in far[0]])
        for bit in range(bits):
            stats = stats + exchange(stats, "tensor", 1 << bit)
        one_parts = gather_first(far_rows)

        def experts(parts, *earlier):
            turn = ordered(index, *earlier)
            return expert_parts(
                turn, [parts[j] for j in range(part_count)], gain, *weights, split
            )

        near_outs = experts(near_parts, far_rows)
        one_parts = gather_parts(ordered(one_parts, near_outs), core_bits)
        far_rows = stack([arrived[k] for k in far[1]], near_outs)
        one_outs = experts(one_parts, near_outs, far_rows)
        two_parts = gather_parts(gather_first(far_rows), core_bits)
        one_terms = cores_added(one_outs)
        one_pieces = give_back(rest_added(one_terms), far[0], returned)
        two_outs = experts(two_parts, one_pieces)
        two_terms = cores_added(two_outs)
        near_terms = cores_added(ordered(near_outs, one_outs))
        near_terms = rest_added(ordered(near_terms, two_terms))
        two_terms = rest_added(two_terms)
        following = None
        if layer_idx + 1 < LAYERS:
            following = [norm_gain[layer_idx + 1 : layer_idx + 2], router_rows[layer_idx + 1]]
            later = ordered(table, two_outs)
            gate_w = in_weights(gate_codes, gate_scales, later, layer_idx + 1)
            two_terms = ordered(two_terms, gate_w)
            two_pieces = give_back(two_terms, far[1], returned)
            later = ordered(table, two_pieces)
            up_w = in_weights(up_codes, up_scales, later, layer_idx + 1)
            near_terms = ordered(near_terms, up_w)
            give_back(near_terms, near, returned)
            down_w = out_weights(down_codes, ordered(down_scales, near_terms), layer_idx + 1)
            weights = (gate_w, up_w, down_w)
            me = ordered(me, weights)
        else:
            two_pieces = give_back(two_terms, far[1], returned)
            give_back(ordered(near_terms, two_pieces), near, returned)
        results = combine(
            me, routes_rows, picks, stats, stream, returned, full_width, following
        )
        if following is None:
            return results[0]
        stream, stats, *slots = results


def solution(mesh):
    in_specs = (
        P("expert", "tensor"),
        P("expert", None),
        P(None, "tensor"),
        P(None, "tensor", None),
        P(None, "expert", None, "tensor"),
        P(None, "expert", None, "tensor"),
        P(None, "expert", None, "tensor"),
        P(None, "expert", None, "tensor"),
        P(None, "expert", "tensor", None),
        P(None, "expert", "tensor", None),
    )
    out_specs = P("expert", "tensor")
    return jax.shard_map(
        per_device, mesh=mesh, in_specs=in_specs, out_specs=out_specs, check_vma=False
    )
```

```python
import functools
import math

import jax
import jax.numpy as jnp
import numpy as np
from jax import lax
from jax.experimental import pallas as pl
from jax.experimental.pallas import tpu as pltpu
from jax.sharding import PartitionSpec as P

LAYERS = 2
GROUP = 128
BLOCK = 256
MIB = 1 << 20
FIRST = 8
SECOND = 64
NT = (((1,), (1,)), ((), ()))
TN = (((0,), (0,)), ((), ()))


def exchange(shard, axis, mask):
    return lax.ppermute(shard, axis, [(i, i ^ mask) for i in range(lax.axis_size(axis))])


def block_table():
    index = np.arange(BLOCK)
    order = np.concatenate([index[0::2], index[1::2]])
    common = index[:, None] & order[None, :]
    ones = np.array([bin(v).count("1") for v in range(BLOCK)])[common]
    return np.where(ones % 2 == 1, -1.0, 1.0).astype(np.float32)


def split_table(width):
    table = np.zeros((width, width), np.float32)
    for unit in range(width):
        table[unit, unit % 2 * (width // 2) + unit // 2] = 1.0
    return table


def power(exponents):
    return (1 << (16 - exponents)).astype(jnp.float32) * (1.0 / 65536.0)


SHORT = pl.CostEstimate(flops=1000, bytes_accessed=1000, transcendentals=0)


def butterfly(rows, start):
    stride = start
    while stride < len(rows):
        for b in range(len(rows)):
            if b & stride == 0:
                low, high = rows[b], rows[b + stride]
                rows[b], rows[b + stride] = low + high, low - high
        stride *= 2


def in_weights_kernel(first_steps, words_ref, scales_ref, table_ref, out_ref, sums_ref):
    half = BLOCK // 2
    words_group = GROUP // 2
    groups_block = BLOCK // GROUP
    step = pl.program_id(0)
    width = words_ref.shape[3]
    block_count = out_ref.shape[0]

    @pl.when(step < first_steps)
    def _():
        sums = []
        for q in range(FIRST):
            words = words_ref[0, 0, q * half : (q + 1) * half, :]
            pieces = []
            for shift in (0, 4):
                codes = ((words >> shift) & 15).astype(jnp.float32) - 8.0
                for g in range(groups_block):
                    at = q * groups_block + g
                    factor = power(scales_ref[0, 0, at : at + 1, :])
                    pieces.append(codes[g * words_group : (g + 1) * words_group] * factor)
            block = jnp.concatenate(pieces, axis=0).astype(jnp.bfloat16)
            sums.append(jnp.dot(table_ref[...], block, preferred_element_type=jnp.float32))
        butterfly(sums, 1)
        for q in range(FIRST):
            sums_ref[step * FIRST + q] = sums[q]

    @pl.when(step >= first_steps)
    def _():
        base = (step - first_steps) * SECOND
        for r in range(0, SECOND, 16):
            for c in range(0, width, 128):
                for q in range(FIRST):
                    rows = [
                        sums_ref[b * FIRST + q, pl.ds(pl.multiple_of(base + r, 16), 16), c : c + 128]
                        for b in range(block_count // FIRST)
                    ]
                    butterfly(rows, 1)
                    for b, row in enumerate(rows):
                        out_ref[b * FIRST + q, r : r + 16, c : c + 128] = row.astype(jnp.bfloat16)


def in_weights(words, scales, table, layer_idx):
    _, _, word_rows, width = words.shape
    full = 2 * word_rows
    block_count = full // BLOCK
    first_steps = block_count // FIRST
    word_tile = FIRST * BLOCK // 2
    group_tile = FIRST * BLOCK // GROUP
    out = pl.pallas_call(
        functools.partial(in_weights_kernel, first_steps),
        grid=(first_steps + BLOCK // SECOND,),
        in_specs=[
            pl.BlockSpec(
                (1, 1, word_tile, width),
                lambda i: (layer_idx, 0, jnp.minimum(i, first_steps - 1), 0),
            ),
            pl.BlockSpec(
                (1, 1, group_tile, width),
                lambda i: (layer_idx, 0, jnp.minimum(i, first_steps - 1), 0),
            ),
            pl.BlockSpec((BLOCK, BLOCK), lambda i: (0, 0)),
        ],
        out_specs=pl.BlockSpec(
            (block_count, SECOND, width), lambda i: (0, jnp.maximum(i - first_steps, 0), 0)
        ),
        out_shape=jax.ShapeDtypeStruct((block_count, BLOCK, width), jnp.bfloat16),
        scratch_shapes=[pltpu.VMEM((block_count, BLOCK, width), jnp.float32)],
        compiler_params=pltpu.CompilerParams(vmem_limit_bytes=54 * MIB),
        cost_estimate=SHORT,
        name="in_weights",
    )(words, scales, table)
    return out.reshape(full, width)


def out_weights_kernel(words_ref, scales_ref, out_ref):
    words = words_ref[0, 0]
    word_rows = words.shape[0]
    words_group = GROUP // 2
    for part, shift in enumerate((0, 4)):
        codes = ((words >> shift) & 15).astype(jnp.float32) - 8.0
        for g in range(word_rows // words_group):
            factor = power(scales_ref[0, 0, pl.ds(g, 1), :])
            out_ref[pl.ds(part * word_rows + g * words_group, words_group), :] = (
                codes[g * words_group : (g + 1) * words_group] * factor
            ).astype(jnp.bfloat16)


def out_weights(words, scales, layer_idx):
    _, _, word_rows, width = words.shape
    groups = scales.shape[2]
    tile = width // 2
    return pl.pallas_call(
        out_weights_kernel,
        grid=(width // tile,),
        in_specs=[
            pl.BlockSpec((1, 1, word_rows, tile), lambda c: (layer_idx, 0, 0, c)),
            pl.BlockSpec((1, 1, groups, tile), lambda c: (layer_idx, 0, 0, c)),
        ],
        out_specs=pl.BlockSpec((2 * word_rows, tile), lambda c: (0, c)),
        out_shape=jax.ShapeDtypeStruct((2 * word_rows, width), jnp.bfloat16),
        compiler_params=pltpu.CompilerParams(vmem_limit_bytes=54 * MIB),
        cost_estimate=SHORT,
        name="out_weights",
    )(words, scales)


def expert_kernel(part_count, full_width, index_ref, *refs):
    x_refs, refs = refs[:part_count], refs[part_count:]
    gain_refs, refs = refs[:part_count], refs[part_count:]
    split_ref, gate_hbm, up_hbm, down_hbm = refs[:4]
    out_refs, refs = refs[4 : 4 + part_count], refs[4 + part_count :]
    gate_ref, up_ref, down_ref, gate_sem, up_sem, down_sem = refs
    width = x_refs[0].shape[1]
    copies = [[], [], []]
    for j in range(part_count):
        at = pl.ds(pl.multiple_of((index_ref[0] ^ j) * width, width), width)
        copies[0].append(
            pltpu.make_async_copy(gate_hbm.at[at, :], gate_ref.at[j], gate_sem.at[j])
        )
        copies[1].append(pltpu.make_async_copy(up_hbm.at[at, :], up_ref.at[j], up_sem.at[j]))
        copies[2].append(
            pltpu.make_async_copy(down_hbm.at[:, at], down_ref.at[j], down_sem.at[j])
        )
    for j in range(part_count):
        copies[0][j].start()
        copies[1][j].start()
    for j in range(part_count):
        copies[2][j].start()
    gate = up = square = None
    for j in range(part_count):
        wide = x_refs[j][...].astype(jnp.float32)
        rows = (wide * gain_refs[j][...]).astype(jnp.bfloat16)
        part = jnp.sum(wide * wide, axis=1, keepdims=True)
        square = part if j == 0 else square + part
        copies[0][j].wait()
        part = jnp.dot(rows, gate_ref[j], preferred_element_type=jnp.float32)
        gate = part if j == 0 else gate + part
        copies[1][j].wait()
        part = jnp.dot(rows, up_ref[j], preferred_element_type=jnp.float32)
        up = part if j == 0 else up + part
    scale = lax.rsqrt(square / full_width + 1e-05) * (1.0 / math.sqrt(full_width))
    gate = gate * scale
    act = (gate / (1.0 + jnp.exp(-gate))) * (up * scale)
    act = jnp.dot(
        act.astype(jnp.bfloat16), split_ref[...], preferred_element_type=jnp.float32
    ).astype(jnp.bfloat16)
    for j in range(part_count):
        copies[2][j].wait()
        out_refs[j][...] = jnp.dot(
            act, down_ref[j], preferred_element_type=jnp.float32
        ).astype(jnp.bfloat16)


def expert_parts(index, parts, gains, gate_w, up_w, down_w, split):
    part_count = len(parts)
    row_count, width = parts[0].shape
    full_width, hidden = gate_w.shape
    vmem = pl.BlockSpec(memory_space=pltpu.VMEM)
    hbm = pl.BlockSpec(memory_space=pltpu.HBM)
    return pl.pallas_call(
        functools.partial(expert_kernel, part_count, full_width),
        in_specs=[pl.BlockSpec(memory_space=pltpu.SMEM)]
        + [vmem] * (2 * part_count + 1)
        + [hbm] * 3,
        out_specs=[vmem] * part_count,
        out_shape=[jax.ShapeDtypeStruct((row_count, width), jnp.bfloat16)] * part_count,
        scratch_shapes=[
            pltpu.VMEM((part_count, width, hidden), jnp.bfloat16),
            pltpu.VMEM((part_count, width, hidden), jnp.bfloat16),
            pltpu.VMEM((part_count, hidden, width), jnp.bfloat16),
            pltpu.SemaphoreType.DMA((part_count,)),
            pltpu.SemaphoreType.DMA((part_count,)),
            pltpu.SemaphoreType.DMA((part_count,)),
        ],
        compiler_params=pltpu.CompilerParams(vmem_limit_bytes=36 * MIB),
        cost_estimate=SHORT,
        name="expert_parts",
    )(index, *parts, *gains, split, gate_w, up_w, down_w)


def add_split_kernel(term_count, *refs):
    total = refs[0][...].astype(jnp.float32)
    for term in refs[1:term_count]:
        total = total + term[...].astype(jnp.float32)
    at = 0
    for out in refs[term_count:]:
        rows = out.shape[0]
        out[...] = total[at : at + rows].astype(jnp.bfloat16)
        at += rows


def add_split(terms, piece_rows):
    row_count, width = terms[0].shape
    return pl.pallas_call(
        functools.partial(add_split_kernel, len(terms)),
        out_shape=[
            jax.ShapeDtypeStruct((piece_rows, width), jnp.bfloat16)
            for _ in range(row_count // piece_rows)
        ],
        compiler_params=pltpu.CompilerParams(vmem_limit_bytes=32 * MIB),
        cost_estimate=SHORT,
        name="add_split",
    )(*terms)


def make_stats(stream, gain, router):
    scaled = (stream * gain).astype(jnp.bfloat16)
    logits = lax.dot_general(router, scaled, NT, preferred_element_type=jnp.float32)
    squares = stream * stream
    high = squares.astype(jnp.bfloat16)
    low = (squares - high.astype(jnp.float32)).astype(jnp.bfloat16)
    ones = jnp.ones((8, stream.shape[1]), jnp.bfloat16)
    square = lax.dot_general(ones, high, NT, preferred_element_type=jnp.float32) + lax.dot_general(
        ones, low, NT, preferred_element_type=jnp.float32
    )
    return logits, square


def fill_slots(picks, rows, slot_refs):
    gathered = jnp.dot(picks, rows, preferred_element_type=jnp.float32)
    capacity = slot_refs[0].shape[0]
    for k, out in enumerate(slot_refs):
        out[...] = gathered[k * capacity : (k + 1) * capacity].astype(jnp.bfloat16)


def enter_kernel(expert_count, me_ref, routes_ref, tokens_ref, gain_ref, router_ref, *refs):
    picks_ref, stats_ref = refs[:2]
    slot_refs = refs[2:]
    token_count = tokens_ref.shape[0]
    capacity = slot_refs[0].shape[0]
    relative = lax.broadcasted_iota(jnp.int32, (expert_count, token_count), 0) ^ me_ref[0]
    first, second = routes_ref[0:1, :], routes_ref[1:2, :]
    member = ((relative == first) | (relative == second)).astype(jnp.float32)
    before = lax.broadcasted_iota(jnp.int32, (token_count, token_count), 0)
    after = lax.broadcasted_iota(jnp.int32, (token_count, token_count), 1)
    earlier = (before < after).astype(jnp.bfloat16)
    ranks = jnp.dot(member.astype(jnp.bfloat16), earlier, preferred_element_type=jnp.float32)
    position = lax.broadcasted_iota(jnp.int32, (capacity, token_count), 0).astype(jnp.float32)
    pieces = [
        jnp.where(position == ranks[k : k + 1, :], member[k : k + 1, :], 0.0)
        for k in range(expert_count)
    ]
    picks = jnp.concatenate(pieces, axis=0).astype(jnp.bfloat16)
    picks_ref[...] = picks
    tokens = tokens_ref[...]
    fill_slots(picks, tokens, slot_refs)
    logits, square = make_stats(tokens.astype(jnp.float32), gain_ref[...], router_ref[...])
    stats_ref[0:expert_count, :] = logits
    stats_ref[expert_count:, :] = square


def enter(me, routes, tokens, gain, router, capacity):
    token_count, width = tokens.shape
    expert_count = router.shape[0]
    vmem = pl.BlockSpec(memory_space=pltpu.VMEM)
    return pl.pallas_call(
        functools.partial(enter_kernel, expert_count),
        in_specs=[pl.BlockSpec(memory_space=pltpu.SMEM)] + [vmem] * 4,
        out_shape=[
            jax.ShapeDtypeStruct((expert_count * capacity, token_count), jnp.bfloat16),
            jax.ShapeDtypeStruct((expert_count + 8, token_count), jnp.float32),
        ]
        + [jax.ShapeDtypeStruct((capacity, width), jnp.bfloat16)] * expert_count,
        compiler_params=pltpu.CompilerParams(vmem_limit_bytes=32 * MIB),
        cost_estimate=SHORT,
        name="enter",
    )(me, routes, tokens, gain, router)


def combine_kernel(expert_count, piece_count, full_width, last, me_ref, *refs):
    routes_ref, picks_ref, stats_ref, stream_ref = refs[:4]
    piece_refs = refs[4 : 4 + piece_count]
    rest = refs[4 + piece_count :]
    token_count = stream_ref.shape[0]
    capacity = picks_ref.shape[0] // expert_count
    first, second = routes_ref[0:1, :], routes_ref[1:2, :]
    logits = stats_ref[0:expert_count, :]
    scale = lax.rsqrt(stats_ref[expert_count : expert_count + 1, :] / full_width + 1e-05)
    expert = lax.broadcasted_iota(jnp.int32, (expert_count, token_count), 0)
    first_logit = jnp.sum(jnp.where(expert == first, logits, 0.0), axis=0, keepdims=True)
    second_logit = jnp.sum(jnp.where(expert == second, logits, 0.0), axis=0, keepdims=True)
    first_weight = 1.0 / (1.0 + jnp.exp((second_logit - first_logit) * scale))
    second_weight = 1.0 - first_weight
    relative = expert ^ me_ref[0]
    weight = jnp.where(relative == first, first_weight, 0.0) + jnp.where(
        relative == second, second_weight, 0.0
    )
    picks = picks_ref[...]
    wide_picks = picks.astype(jnp.float32)
    weighted = jnp.concatenate(
        [
            wide_picks[k * capacity : (k + 1) * capacity] * weight[k : k + 1, :]
            for k in range(expert_count)
        ],
        axis=0,
    )
    high = weighted.astype(jnp.bfloat16)
    low = (weighted - high.astype(jnp.float32)).astype(jnp.bfloat16)
    outs = [piece[...] for piece in piece_refs]
    outs = outs[0] if len(outs) == 1 else jnp.concatenate(outs, axis=0)
    added = lax.dot_general(high, outs, TN, preferred_element_type=jnp.float32)
    added = added + lax.dot_general(low, outs, TN, preferred_element_type=jnp.float32)
    stream = stream_ref[...].astype(jnp.float32) + added
    if last:
        rest[0][...] = stream.astype(jnp.bfloat16)
        return
    gain_ref, router_ref, next_ref, next_stats_ref = rest[:4]
    next_ref[...] = stream
    fill_slots(picks, stream.astype(jnp.bfloat16), rest[4:])
    logits, square = make_stats(stream, gain_ref[...], router_ref[...])
    next_stats_ref[0:expert_count, :] = logits
    next_stats_ref[expert_count:, :] = square


def combine(me, routes, picks, stats, stream, pieces, full_width, following):
    token_count, width = stream.shape
    expert_count = stats.shape[0] - 8
    capacity = picks.shape[0] // expert_count
    if capacity % 16:
        pieces = [jnp.concatenate(pieces, axis=0)]
    vmem = pl.BlockSpec(memory_space=pltpu.VMEM)
    operands = [routes, picks, stats, stream, *pieces]
    if following is None:
        out_shape = [jax.ShapeDtypeStruct((token_count, width), jnp.bfloat16)]
    else:
        operands += following
        out_shape = [
            jax.ShapeDtypeStruct((token_count, width), jnp.float32),
            jax.ShapeDtypeStruct(stats.shape, jnp.float32),
        ] + [jax.ShapeDtypeStruct((capacity, width), jnp.bfloat16)] * expert_count
    return pl.pallas_call(
        functools.partial(
            combine_kernel, expert_count, len(pieces), full_width, following is None
        ),
        in_specs=[pl.BlockSpec(memory_space=pltpu.SMEM)] + [vmem] * len(operands),
        out_shape=out_shape,
        compiler_params=pltpu.CompilerParams(vmem_limit_bytes=32 * MIB),
        cost_estimate=SHORT,
        name="combine",
    )(me, *operands)


def ordered(value, *earlier):
    return lax.optimization_barrier((value, earlier))[0]


def gather_parts(parts, bits):
    parts = dict(parts)
    for bit in bits:
        for j in sorted(parts):
            parts[j ^ 1 << bit] = exchange(parts[j], "tensor", 1 << bit)
    return parts


def reduce_parts(terms, bit):
    kept = {j: list(parts) for j, parts in terms.items() if not j >> bit & 1}
    for j, parts in terms.items():
        if j >> bit & 1:
            total = parts[0]
            if len(parts) > 1:
                total = sum(part.astype(jnp.float32) for part in parts).astype(jnp.bfloat16)
            kept[j ^ 1 << bit].append(exchange(total, "tensor", 1 << bit))
    return kept


def settle(terms):
    return {
        j: parts
        if j == 0 or len(parts) == 1
        else [sum(part.astype(jnp.float32) for part in parts).astype(jnp.bfloat16)]
        for j, parts in terms.items()
    }


def per_device(
    tokens,
    routes,
    norm_gain,
    router_weight,
    gate_codes,
    gate_scales,
    up_codes,
    up_scales,
    down_codes,
    down_scales,
):
    part_count = lax.axis_size("tensor")
    expert_count = lax.axis_size("expert")
    bits = part_count.bit_length() - 1
    token_count, width = tokens.shape
    full_width = width * part_count
    hidden = gate_codes.shape[3]
    capacity = 3 * token_count // expert_count
    me = lax.axis_index("expert").astype(jnp.int32).reshape(1)
    index = lax.axis_index("tensor").astype(jnp.int32).reshape(1)
    table = jnp.asarray(block_table(), jnp.bfloat16)
    split = jnp.asarray(split_table(hidden), jnp.bfloat16)
    routes_rows = routes.T
    router_rows = jnp.swapaxes(router_weight, 1, 2)

    picks, stats, *slots = enter(
        me, routes_rows, tokens, norm_gain[0:1], router_rows[0], capacity
    )
    quarter = expert_count // 4
    near = list(range(2 * quarter))
    far = [list(range(2 * quarter, 3 * quarter)), list(range(3 * quarter, 4 * quarter))]
    first_bits, core_bits = list(reversed(range(1, bits))), [0]
    stream = tokens

    def stack(pieces, *earlier):
        return jnp.concatenate(ordered(pieces, *earlier), axis=0)

    def gather_first(rows):
        return gather_parts({0: rows}, first_bits)

    def cores_added(outs):
        return settle(reduce_parts({j: [part] for j, part in enumerate(outs)}, 0))

    def rest_added(terms):
        for bit in range(1, bits):
            terms = reduce_parts(terms, bit)
        return terms[0]

    def give_back(terms, chunk, returned):
        pieces = add_split(terms, capacity)
        for k, piece in zip(chunk, pieces):
            returned[k] = piece if k == 0 else exchange(piece, "expert", k)
        return pieces

    weights = whole_gain = None
    for layer_idx in range(LAYERS):
        arrived = {0: slots[0]}
        for k in near[1:] + far[0]:
            arrived[k] = exchange(slots[k], "expert", k)
        returned = [None] * expert_count
        near_rows = stack([arrived[k] for k in near])
        near_parts = gather_first(near_rows)
        for k in far[1]:
            arrived[k] = exchange(ordered(slots[k], near_rows), "expert", k)
        if weights is None:
            later = ordered(table, near_rows)
            gate_w = in_weights(gate_codes, gate_scales, later, layer_idx)
            whole_gain = gather_parts({0: ordered(norm_gain, gate_w)}, first_bits + core_bits)
            near_parts = ordered(near_parts, gate_w)
            far_rows = stack([arrived[k] for k in far[0]], gate_w)
            later = ordered(table, near_parts, far_rows)
            near_parts = gather_parts(near_parts, core_bits)
            one_parts = gather_first(far_rows)
            up_w = in_weights(up_codes, up_scales, later, layer_idx)
            one_parts = ordered(one_parts, up_w)
            down_w = out_weights(down_codes, ordered(down_scales, up_w), layer_idx)
            weights = (gate_w, up_w, down_w)
        else:
            near_parts = gather_parts(near_parts, core_bits)
            far_rows = stack([arrived[k] for k in far[0]])
            one_parts = gather_first(far_rows)
        gains = [whole_gain[j][layer_idx : layer_idx + 1] for j in range(part_count)]

        def experts(parts, *earlier):
            turn = ordered(index, *earlier)
            return expert_parts(
                turn, [parts[j] for j in range(part_count)], gains, *weights, split
            )

        near_outs = experts(near_parts, far_rows)
        one_parts = gather_parts(ordered(one_parts, near_outs), core_bits)
        one_outs = experts(one_parts, near_outs)
        far_rows = stack([arrived[k] for k in far[1]], one_outs)
        two_parts = gather_parts(gather_first(far_rows), core_bits)
        one_terms = cores_added(one_outs)
        one_pieces = give_back(rest_added(one_terms), far[0], returned)
        two_outs = experts(two_parts, one_pieces)
        two_terms = rest_added(cores_added(two_outs))
        near_terms = cores_added(ordered(near_outs, two_outs))
        stats = ordered(stats, two_outs)
        for bit in range(bits):
            stats = stats + exchange(stats, "tensor", 1 << bit)
        following = None
        if layer_idx + 1 < LAYERS:
            following = [norm_gain[layer_idx + 1 : layer_idx + 2], router_rows[layer_idx + 1]]
            later = ordered(table, near_terms)
            gate_w = in_weights(gate_codes, gate_scales, later, layer_idx + 1)
            two_terms = ordered(two_terms, gate_w)
            two_pieces = give_back(two_terms, far[1], returned)
            near_terms = rest_added(ordered(near_terms, two_terms))
            later = ordered(table, two_pieces)
            up_w = in_weights(up_codes, up_scales, later, layer_idx + 1)
            near_terms = ordered(near_terms, up_w)
            near_pieces = give_back(near_terms, near, returned)
            later = ordered(down_scales, near_pieces)
            down_w = out_weights(down_codes, later, layer_idx + 1)
            weights = (gate_w, up_w, down_w)
            me = ordered(me, weights)
        else:
            near_terms = rest_added(ordered(near_terms, two_terms))
            two_pieces = give_back(two_terms, far[1], returned)
            give_back(ordered(near_terms, two_pieces), near, returned)
        results = combine(
            me, routes_rows, picks, stats, stream, returned, full_width, following
        )
        if following is None:
            return results[0]
        stream, stats, *slots = results


def solution(mesh):
    in_specs = (
        P("expert", "tensor"),
        P("expert", None),
        P(None, "tensor"),
        P(None, "tensor", None),
        P(None, "expert", None, "tensor"),
        P(None, "expert", None, "tensor"),
        P(None, "expert", None, "tensor"),
        P(None, "expert", None, "tensor"),
        P(None, "expert", "tensor", None),
        P(None, "expert", "tensor", None),
    )
    out_specs = P("expert", "tensor")
    return jax.shard_map(
        per_device, mesh=mesh, in_specs=in_specs, out_specs=out_specs, check_vma=False
    )
```

```python
import functools
import math

import jax
import jax.numpy as jnp
import numpy as np
from jax import lax
from jax.experimental import pallas as pl
from jax.experimental.pallas import tpu as pltpu
from jax.sharding import PartitionSpec as P

LAYERS = 2
GROUP = 128
BLOCK = 256
MIB = 1 << 20
FIRST = 8
SECOND = 64
PIECES = 3
NT = (((1,), (1,)), ((), ()))
TN = (((0,), (0,)), ((), ()))


def exchange(shard, axis, mask):
    return lax.ppermute(shard, axis, [(i, i ^ mask) for i in range(lax.axis_size(axis))])


def block_table():
    index = np.arange(BLOCK)
    order = np.concatenate([index[0::2], index[1::2]])
    common = index[:, None] & order[None, :]
    ones = np.array([bin(v).count("1") for v in range(BLOCK)])[common]
    return np.where(ones % 2 == 1, -1.0, 1.0).astype(np.float32)


def split_table(width):
    table = np.zeros((width, width), np.float32)
    for unit in range(width):
        table[unit, unit % 2 * (width // 2) + unit // 2] = 1.0
    return table


def power(exponents):
    return (1 << (16 - exponents)).astype(jnp.float32) * (1.0 / 65536.0)


SHORT = pl.CostEstimate(flops=1000, bytes_accessed=1000, transcendentals=0)


def butterfly(rows, start):
    stride = start
    while stride < len(rows):
        for b in range(len(rows)):
            if b & stride == 0:
                low, high = rows[b], rows[b + stride]
                rows[b], rows[b + stride] = low + high, low - high
        stride *= 2


def in_weights_kernel(first_steps, words_ref, scales_ref, table_ref, out_ref, sums_ref):
    half = BLOCK // 2
    words_group = GROUP // 2
    groups_block = BLOCK // GROUP
    step = pl.program_id(0)
    width = words_ref.shape[3]
    block_count = out_ref.shape[0]

    @pl.when(step < first_steps)
    def _():
        sums = []
        for q in range(FIRST):
            words = words_ref[0, 0, q * half : (q + 1) * half, :]
            pieces = []
            for shift in (0, 4):
                codes = ((words >> shift) & 15).astype(jnp.float32) - 8.0
                for g in range(groups_block):
                    at = q * groups_block + g
                    factor = power(scales_ref[0, 0, at : at + 1, :])
                    pieces.append(codes[g * words_group : (g + 1) * words_group] * factor)
            block = jnp.concatenate(pieces, axis=0).astype(jnp.bfloat16)
            sums.append(jnp.dot(table_ref[...], block, preferred_element_type=jnp.float32))
        butterfly(sums, 1)
        for q in range(FIRST):
            sums_ref[step * FIRST + q] = sums[q]

    @pl.when(step >= first_steps)
    def _():
        base = (step - first_steps) * SECOND
        for r in range(0, SECOND, 16):
            for c in range(0, width, 128):
                for q in range(FIRST):
                    rows = [
                        sums_ref[b * FIRST + q, pl.ds(pl.multiple_of(base + r, 16), 16), c : c + 128]
                        for b in range(block_count // FIRST)
                    ]
                    butterfly(rows, 1)
                    for b, row in enumerate(rows):
                        out_ref[b * FIRST + q, r : r + 16, c : c + 128] = row.astype(jnp.bfloat16)


def in_weights(words, scales, table, layer_idx):
    _, _, word_rows, width = words.shape
    full = 2 * word_rows
    block_count = full // BLOCK
    first_steps = block_count // FIRST
    word_tile = FIRST * BLOCK // 2
    group_tile = FIRST * BLOCK // GROUP
    out = pl.pallas_call(
        functools.partial(in_weights_kernel, first_steps),
        grid=(first_steps + BLOCK // SECOND,),
        in_specs=[
            pl.BlockSpec(
                (1, 1, word_tile, width),
                lambda i: (layer_idx, 0, jnp.minimum(i, first_steps - 1), 0),
            ),
            pl.BlockSpec(
                (1, 1, group_tile, width),
                lambda i: (layer_idx, 0, jnp.minimum(i, first_steps - 1), 0),
            ),
            pl.BlockSpec((BLOCK, BLOCK), lambda i: (0, 0)),
        ],
        out_specs=pl.BlockSpec(
            (block_count, SECOND, width), lambda i: (0, jnp.maximum(i - first_steps, 0), 0)
        ),
        out_shape=jax.ShapeDtypeStruct((block_count, BLOCK, width), jnp.bfloat16),
        scratch_shapes=[pltpu.VMEM((block_count, BLOCK, width), jnp.float32)],
        compiler_params=pltpu.CompilerParams(vmem_limit_bytes=54 * MIB),
        cost_estimate=SHORT,
        name="in_weights",
    )(words, scales, table)
    return out.reshape(full, width)


def out_weights_kernel(words_ref, scales_ref, out_ref):
    words = words_ref[0, 0]
    word_rows = words.shape[0]
    words_group = GROUP // 2
    for part, shift in enumerate((0, 4)):
        codes = ((words >> shift) & 15).astype(jnp.float32) - 8.0
        for g in range(word_rows // words_group):
            factor = power(scales_ref[0, 0, pl.ds(g, 1), :])
            out_ref[pl.ds(part * word_rows + g * words_group, words_group), :] = (
                codes[g * words_group : (g + 1) * words_group] * factor
            ).astype(jnp.bfloat16)


def out_weights(words, scales, layer_idx):
    _, _, word_rows, width = words.shape
    groups = scales.shape[2]
    tile = width // 2
    return pl.pallas_call(
        out_weights_kernel,
        grid=(width // tile,),
        in_specs=[
            pl.BlockSpec((1, 1, word_rows, tile), lambda c: (layer_idx, 0, 0, c)),
            pl.BlockSpec((1, 1, groups, tile), lambda c: (layer_idx, 0, 0, c)),
        ],
        out_specs=pl.BlockSpec((2 * word_rows, tile), lambda c: (0, c)),
        out_shape=jax.ShapeDtypeStruct((2 * word_rows, width), jnp.bfloat16),
        compiler_params=pltpu.CompilerParams(vmem_limit_bytes=54 * MIB),
        cost_estimate=SHORT,
        name="out_weights",
    )(words, scales)


def expert_kernel(part_count, full_width, index_ref, *refs):
    x_refs, refs = refs[:part_count], refs[part_count:]
    gain_refs, refs = refs[:part_count], refs[part_count:]
    split_ref, gate_hbm, up_hbm, down_hbm = refs[:4]
    out_refs, refs = refs[4:6], refs[6:]
    gate_ref, up_ref, down_ref, gate_sem, up_sem, down_sem = refs
    width = x_refs[0].shape[1]
    copies = [[], [], []]
    for j in range(part_count):
        at = pl.ds(pl.multiple_of((index_ref[0] ^ j) * width, width), width)
        copies[0].append(
            pltpu.make_async_copy(gate_hbm.at[at, :], gate_ref.at[j], gate_sem.at[j])
        )
        copies[1].append(pltpu.make_async_copy(up_hbm.at[at, :], up_ref.at[j], up_sem.at[j]))
        copies[2].append(
            pltpu.make_async_copy(down_hbm.at[:, at], down_ref.at[j], down_sem.at[j])
        )
    for j in range(part_count):
        copies[0][j].start()
        copies[1][j].start()
    for j in range(part_count):
        copies[2][j].start()
    gate = up = square = None
    for j in range(part_count):
        wide = x_refs[j][...].astype(jnp.float32)
        rows = (wide * gain_refs[j][...]).astype(jnp.bfloat16)
        part = jnp.sum(wide * wide, axis=1, keepdims=True)
        square = part if j == 0 else square + part
        copies[0][j].wait()
        part = jnp.dot(rows, gate_ref[j], preferred_element_type=jnp.float32)
        gate = part if j == 0 else gate + part
        copies[1][j].wait()
        part = jnp.dot(rows, up_ref[j], preferred_element_type=jnp.float32)
        up = part if j == 0 else up + part
    scale = lax.rsqrt(square / full_width + 1e-05) * (1.0 / math.sqrt(full_width))
    gate = gate * scale
    act = (gate / (1.0 + jnp.exp(-gate))) * (up * scale)
    act = jnp.dot(
        act.astype(jnp.bfloat16), split_ref[...], preferred_element_type=jnp.float32
    ).astype(jnp.bfloat16)
    for j in range(part_count):
        copies[2][j].wait()
        out_refs[j % 2][j // 2] = jnp.dot(
            act, down_ref[j], preferred_element_type=jnp.float32
        ).astype(jnp.bfloat16)


def expert_parts(index, parts, gains, gate_w, up_w, down_w, split):
    part_count = len(parts)
    row_count, width = parts[0].shape
    full_width, hidden = gate_w.shape
    vmem = pl.BlockSpec(memory_space=pltpu.VMEM)
    hbm = pl.BlockSpec(memory_space=pltpu.HBM)
    return pl.pallas_call(
        functools.partial(expert_kernel, part_count, full_width),
        in_specs=[pl.BlockSpec(memory_space=pltpu.SMEM)]
        + [vmem] * (2 * part_count + 1)
        + [hbm] * 3,
        out_specs=[vmem] * 2,
        out_shape=[jax.ShapeDtypeStruct((part_count // 2, row_count, width), jnp.bfloat16)] * 2,
        scratch_shapes=[
            pltpu.VMEM((part_count, width, hidden), jnp.bfloat16),
            pltpu.VMEM((part_count, width, hidden), jnp.bfloat16),
            pltpu.VMEM((part_count, hidden, width), jnp.bfloat16),
            pltpu.SemaphoreType.DMA((part_count,)),
            pltpu.SemaphoreType.DMA((part_count,)),
            pltpu.SemaphoreType.DMA((part_count,)),
        ],
        compiler_params=pltpu.CompilerParams(vmem_limit_bytes=36 * MIB),
        cost_estimate=SHORT,
        name="expert_parts",
    )(index, *parts, *gains, split, gate_w, up_w, down_w)


def add_first_kernel(*refs):
    total = refs[0][0].astype(jnp.float32)
    for term in refs[1:-1]:
        total = total + term[0].astype(jnp.float32)
    refs[-1][...] = total.astype(jnp.bfloat16)


def add_first(terms):
    vmem = pl.BlockSpec(memory_space=pltpu.VMEM)
    return pl.pallas_call(
        add_first_kernel,
        in_specs=[vmem] * len(terms),
        out_specs=vmem,
        out_shape=jax.ShapeDtypeStruct(terms[0].shape[1:], jnp.bfloat16),
        compiler_params=pltpu.CompilerParams(vmem_limit_bytes=32 * MIB),
        cost_estimate=SHORT,
        name="add_first",
    )(*terms)


def make_stats(stream, gain, router):
    scaled = (stream * gain).astype(jnp.bfloat16)
    logits = lax.dot_general(router, scaled, NT, preferred_element_type=jnp.float32)
    squares = stream * stream
    high = squares.astype(jnp.bfloat16)
    low = (squares - high.astype(jnp.float32)).astype(jnp.bfloat16)
    ones = jnp.ones((8, stream.shape[1]), jnp.bfloat16)
    square = lax.dot_general(ones, high, NT, preferred_element_type=jnp.float32) + lax.dot_general(
        ones, low, NT, preferred_element_type=jnp.float32
    )
    return logits, square


def fill_slots(picks, rows, slot_refs):
    gathered = jnp.dot(picks, rows, preferred_element_type=jnp.float32)
    at = 0
    for out in slot_refs:
        out[...] = gathered[at : at + out.shape[0]].astype(jnp.bfloat16)
        at += out.shape[0]


def enter_kernel(expert_count, routes_ref, tokens_ref, gain_ref, router_ref, *refs):
    picks_ref, stats_ref = refs[:2]
    slot_refs = refs[2:]
    token_count = tokens_ref.shape[0]
    expert = lax.broadcasted_iota(jnp.int32, (expert_count, token_count), 0)
    first, second = routes_ref[0:1, :], routes_ref[1:2, :]
    member = ((expert == first) | (expert == second)).astype(jnp.float32)
    before = lax.broadcasted_iota(jnp.int32, (token_count, token_count), 0)
    after = lax.broadcasted_iota(jnp.int32, (token_count, token_count), 1)
    earlier = (before < after).astype(jnp.bfloat16)
    ranks = jnp.dot(member.astype(jnp.bfloat16), earlier, preferred_element_type=jnp.float32)
    pieces = []
    at = 0
    for out in slot_refs:
        count = out.shape[0] // expert_count
        position = lax.broadcasted_iota(jnp.int32, (count, token_count), 0) + at
        position = position.astype(jnp.float32)
        pieces += [
            jnp.where(position == ranks[e : e + 1, :], member[e : e + 1, :], 0.0)
            for e in range(expert_count)
        ]
        at += count
    picks = jnp.concatenate(pieces, axis=0).astype(jnp.bfloat16)
    picks_ref[...] = picks
    tokens = tokens_ref[...]
    fill_slots(picks, tokens, slot_refs)
    logits, square = make_stats(tokens.astype(jnp.float32), gain_ref[...], router_ref[...])
    stats_ref[0:expert_count, :] = logits
    stats_ref[expert_count:, :] = square


def slot_shapes(expert_count, capacity, width):
    rows = expert_count * capacity // PIECES
    return [jax.ShapeDtypeStruct((rows, width), jnp.bfloat16)] * PIECES


def enter(routes, tokens, gain, router, capacity):
    token_count, width = tokens.shape
    expert_count = router.shape[0]
    vmem = pl.BlockSpec(memory_space=pltpu.VMEM)
    return pl.pallas_call(
        functools.partial(enter_kernel, expert_count),
        in_specs=[vmem] * 4,
        out_shape=[
            jax.ShapeDtypeStruct((expert_count * capacity, token_count), jnp.bfloat16),
            jax.ShapeDtypeStruct((expert_count + 8, token_count), jnp.float32),
        ]
        + slot_shapes(expert_count, capacity, width),
        compiler_params=pltpu.CompilerParams(vmem_limit_bytes=32 * MIB),
        cost_estimate=SHORT,
        name="enter",
    )(routes, tokens, gain, router)


def combine_kernel(expert_count, piece_count, full_width, last, *refs):
    routes_ref, picks_ref, stats_ref, stream_ref = refs[:4]
    piece_refs = refs[4 : 4 + piece_count]
    rest = refs[4 + piece_count :]
    token_count = stream_ref.shape[0]
    first, second = routes_ref[0:1, :], routes_ref[1:2, :]
    logits = stats_ref[0:expert_count, :]
    scale = lax.rsqrt(stats_ref[expert_count : expert_count + 1, :] / full_width + 1e-05)
    expert = lax.broadcasted_iota(jnp.int32, (expert_count, token_count), 0)
    first_logit = jnp.sum(jnp.where(expert == first, logits, 0.0), axis=0, keepdims=True)
    second_logit = jnp.sum(jnp.where(expert == second, logits, 0.0), axis=0, keepdims=True)
    first_weight = 1.0 / (1.0 + jnp.exp((second_logit - first_logit) * scale))
    second_weight = 1.0 - first_weight
    weight = jnp.where(expert == first, first_weight, 0.0) + jnp.where(
        expert == second, second_weight, 0.0
    )
    picks = picks_ref[...]
    wide_picks = picks.astype(jnp.float32)
    pieces = []
    at = 0
    for piece in piece_refs:
        count = piece.shape[0] // expert_count
        for e in range(expert_count):
            pieces.append(wide_picks[at : at + count] * weight[e : e + 1, :])
            at += count
    weighted = jnp.concatenate(pieces, axis=0)
    high = weighted.astype(jnp.bfloat16)
    low = (weighted - high.astype(jnp.float32)).astype(jnp.bfloat16)
    outs = jnp.concatenate([piece[...] for piece in piece_refs], axis=0)
    added = lax.dot_general(high, outs, TN, preferred_element_type=jnp.float32)
    added = added + lax.dot_general(low, outs, TN, preferred_element_type=jnp.float32)
    stream = stream_ref[...].astype(jnp.float32) + added
    if last:
        rest[0][...] = stream.astype(jnp.bfloat16)
        return
    gain_ref, router_ref, next_ref, next_stats_ref = rest[:4]
    next_ref[...] = stream
    fill_slots(picks, stream.astype(jnp.bfloat16), rest[4:])
    logits, square = make_stats(stream, gain_ref[...], router_ref[...])
    next_stats_ref[0:expert_count, :] = logits
    next_stats_ref[expert_count:, :] = square


def combine(routes, picks, stats, stream, pieces, full_width, following):
    token_count, width = stream.shape
    expert_count = stats.shape[0] - 8
    capacity = picks.shape[0] // expert_count
    vmem = pl.BlockSpec(memory_space=pltpu.VMEM)
    operands = [routes, picks, stats, stream, *pieces]
    if following is None:
        out_shape = [jax.ShapeDtypeStruct((token_count, width), jnp.bfloat16)]
    else:
        operands += following
        out_shape = [
            jax.ShapeDtypeStruct((token_count, width), jnp.float32),
            jax.ShapeDtypeStruct(stats.shape, jnp.float32),
        ] + slot_shapes(expert_count, capacity, width)
    return pl.pallas_call(
        functools.partial(
            combine_kernel, expert_count, len(pieces), full_width, following is None
        ),
        in_specs=[vmem] * len(operands),
        out_shape=out_shape,
        compiler_params=pltpu.CompilerParams(vmem_limit_bytes=32 * MIB),
        cost_estimate=SHORT,
        name="combine",
    )(*operands)


def ordered(value, *earlier):
    return lax.optimization_barrier((value, earlier))[0]


def gather_parts(parts, bits):
    parts = dict(parts)
    for bit in bits:
        for j in sorted(parts):
            parts[j ^ 1 << bit] = exchange(parts[j], "tensor", 1 << bit)
    return parts


def deal(rows):
    return lax.all_to_all(rows, "expert", split_axis=0, concat_axis=0, tiled=True)


def per_device(
    tokens,
    routes,
    norm_gain,
    router_weight,
    gate_codes,
    gate_scales,
    up_codes,
    up_scales,
    down_codes,
    down_scales,
):
    part_count = lax.axis_size("tensor")
    expert_count = lax.axis_size("expert")
    bits = part_count.bit_length() - 1
    token_count, width = tokens.shape
    full_width = width * part_count
    hidden = gate_codes.shape[3]
    capacity = 3 * token_count // expert_count
    index = lax.axis_index("tensor").astype(jnp.int32).reshape(1)
    table = jnp.asarray(block_table(), jnp.bfloat16)
    split = jnp.asarray(split_table(hidden), jnp.bfloat16)
    routes_rows = routes.T
    router_rows = jnp.swapaxes(router_weight, 1, 2)
    first_bits, core_bits = list(reversed(range(1, bits))), [0]

    def gather_first(rows, *earlier):
        return gather_parts({0: ordered(rows, *earlier)}, first_bits)

    def send_on(arrays):
        total = sum(array[step :: 2 * step].astype(jnp.float32) for array, step in arrays)
        return total.astype(jnp.bfloat16)

    def prepare_in(codes, scales, layer_idx, *earlier):
        return in_weights(codes, scales, ordered(table, *earlier), layer_idx)

    def prepare_out(layer_idx, *earlier):
        return out_weights(down_codes, ordered(down_scales, *earlier), layer_idx)

    picks, stats, *slots = enter(routes_rows, tokens, norm_gain[0:1], router_rows[0], capacity)
    count = len(slots)
    stream = tokens
    whole_gain = gather_parts({0: norm_gain}, first_bits + core_bits)
    weights = None
    for layer_idx in range(LAYERS):
        arrived = [deal(rows) for rows in slots]
        for bit in range(bits):
            stats = stats + exchange(stats, "tensor", 1 << bit)
        parts = [gather_first(arrived[0], stats, whole_gain)]
        if weights is None:
            gate_w = prepare_in(gate_codes, gate_scales, layer_idx, parts[0][0])
            parts.append(gather_first(arrived[1], gate_w))
            parts[0] = gather_parts(ordered(parts[0], gate_w), core_bits)
            up_w = prepare_in(up_codes, up_scales, layer_idx, gate_w, parts[1][0])
            if count > 2:
                parts.append(gather_first(arrived[2], up_w))
            down_w = prepare_out(layer_idx, up_w, parts[-1][0])
            weights = (gate_w, up_w, down_w)
        else:
            parts.append(gather_first(arrived[1], parts[0]))
            parts[0] = gather_parts(parts[0], core_bits)
        gains = [whole_gain[j][layer_idx : layer_idx + 1] for j in range(part_count)]

        def experts(parts, *earlier):
            return expert_parts(
                ordered(index, *earlier),
                [parts[j] for j in range(part_count)],
                gains,
                *weights,
                split,
            )

        returned = []
        held = []
        outs = experts(parts[0], parts[1][0])
        for c in range(count):
            if len(parts) <= c + 2 < count + 1 and c + 2 < count:
                parts.append(gather_first(arrived[c + 2], outs))
            kept, away = outs
            arrays = [(kept, 1), (exchange(away, "tensor", 1), 1)]
            if c + 1 < count:
                parts[c + 1] = gather_parts(ordered(parts[c + 1], outs), core_bits)
            for bit in range(1, bits):
                leaving = send_on(arrays)
                if c + 2 < count:
                    leaving = ordered(leaving, parts[c + 2][0])
                arrays = [(array, 2 * step) for array, step in arrays]
                arrays.append((exchange(leaving, "tensor", 1 << bit), 1))
            held.append([array for array, _ in arrays])
            if c + 1 < count:
                outs = experts(parts[c + 1], leaving)
            else:
                last = leaving
        for c in range(count - 1):
            returned.append(deal(add_first(ordered(held[c], last))))
        following = None
        if layer_idx + 1 < LAYERS:
            following = [norm_gain[layer_idx + 1 : layer_idx + 2], router_rows[layer_idx + 1]]
            gate_w = prepare_in(gate_codes, gate_scales, layer_idx + 1, last)
            total = add_first(ordered(held[-1], gate_w))
            returned.append(deal(total))
            up_w = prepare_in(up_codes, up_scales, layer_idx + 1, total)
            down_w = prepare_out(layer_idx + 1, up_w)
            weights = (gate_w, up_w, down_w)
            stats = ordered(stats, weights)
        else:
            returned.append(deal(add_first(held[-1])))
        results = combine(routes_rows, picks, stats, stream, returned, full_width, following)
        if following is None:
            return results[0]
        stream, stats, *slots = results


def solution(mesh):
    in_specs = (
        P("expert", "tensor"),
        P("expert", None),
        P(None, "tensor"),
        P(None, "tensor", None),
        P(None, "expert", None, "tensor"),
        P(None, "expert", None, "tensor"),
        P(None, "expert", None, "tensor"),
        P(None, "expert", None, "tensor"),
        P(None, "expert", "tensor", None),
        P(None, "expert", "tensor", None),
    )
    out_specs = P("expert", "tensor")
    return jax.shard_map(
        per_device, mesh=mesh, in_specs=in_specs, out_specs=out_specs, check_vma=False
    )
```

```python
import functools
import math

import jax
import jax.numpy as jnp
import numpy as np
from jax import lax
from jax.experimental import pallas as pl
from jax.experimental.pallas import tpu as pltpu
from jax.sharding import PartitionSpec as P

LAYERS = 2
ORDERS = (
    (
        ("Ra", 0), ("G", 1), ("Wg0", 1), ("Rb", 0), ("V0", 1), ("Wd0", 1), ("Wu0", 1),
        ("Rc", 1), ("Ca", 0), ("Ea", 1), ("Cb", 0), ("Cc", 0), ("Ec", 0), ("Xa", 1), ("Xc", 0),
        ("Eb", 0), ("Xb", 0), ("S", 0), ("Wg1", 1), ("Pc", 0), ("Pa", 1), ("Wu1", 0), ("Pb", 1),
        ("V1", 1),
    ),
    (
        ("Nc", 1), ("Na", 0), ("Ra", 1), ("Nb", 1), ("Rb", 1), ("Ca", 1), ("Ea", 1), ("Xa", 1),
        ("v", 0), ("Rc", 0), ("Wd1", 1), ("Cb", 1), ("Pa", 1), ("Eb", 0), ("S", 1), ("Xb", 1),
        ("Cc", 1), ("Ec", 0), ("Pb", 1), ("Xc", 1), ("Pc", 1),
    ),
)
GROUPS = (
    (("a", (0, 1, 2, 3)), ("b", (4, 5)), ("c", (6, 7))),
    (("a", (0, 1, 2, 3)), ("b", (4, 5)), ("c", (6, 7))),
)
GROUP = 128
BLOCK = 256
MIB = 1 << 20
FIRST = 8
SECOND = 64
NT = (((1,), (1,)), ((), ()))
TN = (((0,), (0,)), ((), ()))


def exchange(shard, axis, mask):
    return lax.ppermute(shard, axis, [(i, i ^ mask) for i in range(lax.axis_size(axis))])


def block_table():
    index = np.arange(BLOCK)
    order = np.concatenate([index[0::2], index[1::2]])
    common = index[:, None] & order[None, :]
    ones = np.array([bin(v).count("1") for v in range(BLOCK)])[common]
    return np.where(ones % 2 == 1, -1.0, 1.0).astype(np.float32)


def split_table(width):
    table = np.zeros((width, width), np.float32)
    for unit in range(width):
        table[unit, unit % 2 * (width // 2) + unit // 2] = 1.0
    return table


def power(exponents):
    return (1 << (16 - exponents)).astype(jnp.float32) * (1.0 / 65536.0)


SHORT = pl.CostEstimate(flops=1000, bytes_accessed=1000, transcendentals=0)


def butterfly(rows, start):
    stride = start
    while stride < len(rows):
        for b in range(len(rows)):
            if b & stride == 0:
                low, high = rows[b], rows[b + stride]
                rows[b], rows[b + stride] = low + high, low - high
        stride *= 2


def in_weights_kernel(first_steps, words_ref, scales_ref, table_ref, out_ref, sums_ref):
    half = BLOCK // 2
    words_group = GROUP // 2
    groups_block = BLOCK // GROUP
    step = pl.program_id(0)
    width = words_ref.shape[3]
    block_count = out_ref.shape[0]

    @pl.when(step < first_steps)
    def _():
        sums = []
        for q in range(FIRST):
            words = words_ref[0, 0, q * half : (q + 1) * half, :]
            pieces = []
            for shift in (0, 4):
                codes = ((words >> shift) & 15).astype(jnp.float32) - 8.0
                for g in range(groups_block):
                    at = q * groups_block + g
                    factor = power(scales_ref[0, 0, at : at + 1, :])
                    pieces.append(codes[g * words_group : (g + 1) * words_group] * factor)
            block = jnp.concatenate(pieces, axis=0).astype(jnp.bfloat16)
            sums.append(jnp.dot(table_ref[...], block, preferred_element_type=jnp.float32))
        butterfly(sums, 1)
        for q in range(FIRST):
            sums_ref[step * FIRST + q] = sums[q]

    @pl.when(step >= first_steps)
    def _():
        base = (step - first_steps) * SECOND
        for r in range(0, SECOND, 16):
            for c in range(0, width, 128):
                for q in range(FIRST):
                    rows = [
                        sums_ref[b * FIRST + q, pl.ds(pl.multiple_of(base + r, 16), 16), c : c + 128]
                        for b in range(block_count // FIRST)
                    ]
                    butterfly(rows, 1)
                    for b, row in enumerate(rows):
                        out_ref[b * FIRST + q, r : r + 16, c : c + 128] = row.astype(jnp.bfloat16)


def in_weights(words, scales, table, layer_idx):
    _, _, word_rows, width = words.shape
    full = 2 * word_rows
    block_count = full // BLOCK
    first_steps = block_count // FIRST
    word_tile = FIRST * BLOCK // 2
    group_tile = FIRST * BLOCK // GROUP
    out = pl.pallas_call(
        functools.partial(in_weights_kernel, first_steps),
        grid=(first_steps + BLOCK // SECOND,),
        in_specs=[
            pl.BlockSpec(
                (1, 1, word_tile, width),
                lambda i: (layer_idx, 0, jnp.minimum(i, first_steps - 1), 0),
            ),
            pl.BlockSpec(
                (1, 1, group_tile, width),
                lambda i: (layer_idx, 0, jnp.minimum(i, first_steps - 1), 0),
            ),
            pl.BlockSpec((BLOCK, BLOCK), lambda i: (0, 0)),
        ],
        out_specs=pl.BlockSpec(
            (block_count, SECOND, width), lambda i: (0, jnp.maximum(i - first_steps, 0), 0)
        ),
        out_shape=jax.ShapeDtypeStruct((block_count, BLOCK, width), jnp.bfloat16),
        scratch_shapes=[pltpu.VMEM((block_count, BLOCK, width), jnp.float32)],
        compiler_params=pltpu.CompilerParams(vmem_limit_bytes=54 * MIB),
        cost_estimate=SHORT,
        name="in_weights",
    )(words, scales, table)
    return out.reshape(full, width)


def down_rows_kernel(words_ref, scales_ref, out_ref):
    words = words_ref[0, 0]
    word_rows = words.shape[0]
    words_group = GROUP // 2
    for part, shift in enumerate((0, 4)):
        codes = ((words >> shift) & 15).astype(jnp.float32) - 8.0
        for g in range(word_rows // words_group):
            factor = power(scales_ref[0, 0, pl.ds(g, 1), :])
            out_ref[pl.ds(part * word_rows + g * words_group, words_group), :] = (
                codes[g * words_group : (g + 1) * words_group] * factor
            ).astype(jnp.bfloat16)


def down_rows(words, scales, layer_idx):
    _, _, word_rows, width = words.shape
    groups = scales.shape[2]
    tile = width // 2
    return pl.pallas_call(
        down_rows_kernel,
        grid=(width // tile,),
        in_specs=[
            pl.BlockSpec((1, 1, word_rows, tile), lambda c: (layer_idx, 0, 0, c)),
            pl.BlockSpec((1, 1, groups, tile), lambda c: (layer_idx, 0, 0, c)),
        ],
        out_specs=pl.BlockSpec((2 * word_rows, tile), lambda c: (0, c)),
        out_shape=jax.ShapeDtypeStruct((2 * word_rows, width), jnp.bfloat16),
        compiler_params=pltpu.CompilerParams(vmem_limit_bytes=54 * MIB),
        cost_estimate=SHORT,
        name="out_weights_rows",
    )(words, scales)


def expert_kernel(part_count, full_width, index_ref, *refs):
    x_refs, refs = refs[:part_count], refs[part_count:]
    gain_refs, refs = refs[:part_count], refs[part_count:]
    split_ref, gate_hbm, up_hbm, down_hbm = refs[:4]
    out_refs, refs = refs[4:6], refs[6:]
    gate_ref, up_ref, down_ref, gate_sem, up_sem, down_sem = refs
    width = x_refs[0].shape[1]
    copies = [[], [], []]
    for j in range(part_count):
        at = pl.ds(pl.multiple_of((index_ref[0] ^ j) * width, width), width)
        copies[0].append(
            pltpu.make_async_copy(gate_hbm.at[at, :], gate_ref.at[j], gate_sem.at[j])
        )
        copies[1].append(pltpu.make_async_copy(up_hbm.at[at, :], up_ref.at[j], up_sem.at[j]))
        copies[2].append(
            pltpu.make_async_copy(down_hbm.at[:, at], down_ref.at[j], down_sem.at[j])
        )
    for j in range(part_count):
        copies[0][j].start()
        copies[1][j].start()
    for j in range(part_count):
        copies[2][j].start()
    gate = up = square = None
    for j in range(part_count):
        wide = x_refs[j][...].astype(jnp.float32)
        rows = (wide * gain_refs[j][...]).astype(jnp.bfloat16)
        part = jnp.sum(wide * wide, axis=1, keepdims=True)
        square = part if j == 0 else square + part
        copies[0][j].wait()
        part = jnp.dot(rows, gate_ref[j], preferred_element_type=jnp.float32)
        gate = part if j == 0 else gate + part
        copies[1][j].wait()
        part = jnp.dot(rows, up_ref[j], preferred_element_type=jnp.float32)
        up = part if j == 0 else up + part
    scale = lax.rsqrt(square / full_width + 1e-05) * (1.0 / math.sqrt(full_width))
    gate = gate * scale
    act = (gate / (1.0 + jnp.exp(-gate))) * (up * scale)
    act = jnp.dot(
        act.astype(jnp.bfloat16), split_ref[...], preferred_element_type=jnp.float32
    ).astype(jnp.bfloat16)
    for j in range(part_count):
        copies[2][j].wait()
        out_refs[j % 2][j // 2] = jnp.dot(
            act, down_ref[j], preferred_element_type=jnp.float32
        ).astype(jnp.bfloat16)


def expert_parts(index, parts, gains, gate_w, up_w, down_w, split):
    part_count = len(parts)
    row_count, width = parts[0].shape
    full_width, hidden = gate_w.shape
    vmem = pl.BlockSpec(memory_space=pltpu.VMEM)
    hbm = pl.BlockSpec(memory_space=pltpu.HBM)
    return pl.pallas_call(
        functools.partial(expert_kernel, part_count, full_width),
        in_specs=[pl.BlockSpec(memory_space=pltpu.SMEM)]
        + [vmem] * (2 * part_count + 1)
        + [hbm] * 3,
        out_specs=[vmem] * 2,
        out_shape=[jax.ShapeDtypeStruct((part_count // 2, row_count, width), jnp.bfloat16)] * 2,
        scratch_shapes=[
            pltpu.VMEM((part_count, width, hidden), jnp.bfloat16),
            pltpu.VMEM((part_count, width, hidden), jnp.bfloat16),
            pltpu.VMEM((part_count, hidden, width), jnp.bfloat16),
            pltpu.SemaphoreType.DMA((part_count,)),
            pltpu.SemaphoreType.DMA((part_count,)),
            pltpu.SemaphoreType.DMA((part_count,)),
        ],
        compiler_params=pltpu.CompilerParams(vmem_limit_bytes=36 * MIB),
        cost_estimate=SHORT,
        name="expert_parts",
    )(index, *parts, *gains, split, gate_w, up_w, down_w)


def add_split_kernel(term_count, *refs):
    total = refs[0][0].astype(jnp.float32)
    for term in refs[1:term_count]:
        total = total + term[0].astype(jnp.float32)
    at = 0
    for out in refs[term_count:]:
        rows = out.shape[0]
        out[...] = total[at : at + rows].astype(jnp.bfloat16)
        at += rows


def add_split(terms, piece_rows):
    _, row_count, width = terms[0].shape
    vmem = pl.BlockSpec(memory_space=pltpu.VMEM)
    count = row_count // piece_rows
    return pl.pallas_call(
        functools.partial(add_split_kernel, len(terms)),
        in_specs=[vmem] * len(terms),
        out_specs=[vmem] * count,
        out_shape=[jax.ShapeDtypeStruct((piece_rows, width), jnp.bfloat16)] * count,
        compiler_params=pltpu.CompilerParams(vmem_limit_bytes=32 * MIB),
        cost_estimate=SHORT,
        name="add_split",
    )(*terms)


def out_weights_kernel(word_rows, *refs):
    out_ref = refs[-1]
    words_group = GROUP // 2
    for source, ref in enumerate(refs[:-1]):
        for g in range(word_rows // words_group):
            words = ref[g * words_group : (g + 1) * words_group, :]
            factor = power(ref[word_rows + g : word_rows + g + 1, :])
            for part, shift in enumerate((0, 4)):
                codes = ((words >> shift) & 15).astype(jnp.float32) - 8.0
                at = part * word_rows + g * words_group
                out_ref[source, at : at + words_group, :] = (codes * factor).astype(jnp.bfloat16)


def out_weights(blocks, word_rows):
    width = blocks[0].shape[1]
    vmem = pl.BlockSpec(memory_space=pltpu.VMEM)
    return pl.pallas_call(
        functools.partial(out_weights_kernel, word_rows),
        in_specs=[vmem] * len(blocks),
        out_specs=vmem,
        out_shape=jax.ShapeDtypeStruct((len(blocks), 2 * word_rows, width), jnp.bfloat16),
        compiler_params=pltpu.CompilerParams(vmem_limit_bytes=24 * MIB),
        cost_estimate=SHORT,
        name="out_weights",
    )(*blocks)


def hidden_kernel(part_count, full_width, index_ref, *refs):
    x_refs, refs = refs[:part_count], refs[part_count:]
    gain_refs, refs = refs[:part_count], refs[part_count:]
    split_ref, gate_hbm, up_hbm, out_ref, gate_ref, up_ref, gate_sem, up_sem = refs
    width = x_refs[0].shape[1]
    copies = []
    for j in range(part_count):
        at = pl.ds(pl.multiple_of((index_ref[0] ^ j) * width, width), width)
        copies.append(
            (
                pltpu.make_async_copy(gate_hbm.at[at, :], gate_ref.at[j], gate_sem.at[j]),
                pltpu.make_async_copy(up_hbm.at[at, :], up_ref.at[j], up_sem.at[j]),
            )
        )
        copies[j][0].start()
        copies[j][1].start()
    gate = up = square = None
    for j in range(part_count):
        wide = x_refs[j][...].astype(jnp.float32)
        rows = (wide * gain_refs[j][...]).astype(jnp.bfloat16)
        part = jnp.sum(wide * wide, axis=1, keepdims=True)
        square = part if j == 0 else square + part
        copies[j][0].wait()
        part = jnp.dot(rows, gate_ref[j], preferred_element_type=jnp.float32)
        gate = part if j == 0 else gate + part
        copies[j][1].wait()
        part = jnp.dot(rows, up_ref[j], preferred_element_type=jnp.float32)
        up = part if j == 0 else up + part
    scale = lax.rsqrt(square / full_width + 1e-05) * (1.0 / math.sqrt(full_width))
    gate = gate * scale
    act = (gate / (1.0 + jnp.exp(-gate))) * (up * scale)
    out_ref[...] = jnp.dot(
        act.astype(jnp.bfloat16), split_ref[...], preferred_element_type=jnp.float32
    ).astype(jnp.bfloat16)


def hidden_units(index, parts, gains, gate_w, up_w, split):
    part_count = len(parts)
    row_count, width = parts[0].shape
    full_width, hidden = gate_w.shape
    vmem = pl.BlockSpec(memory_space=pltpu.VMEM)
    hbm = pl.BlockSpec(memory_space=pltpu.HBM)
    return pl.pallas_call(
        functools.partial(hidden_kernel, part_count, full_width),
        in_specs=[pl.BlockSpec(memory_space=pltpu.SMEM)]
        + [vmem] * (2 * part_count + 1)
        + [hbm] * 2,
        out_specs=vmem,
        out_shape=jax.ShapeDtypeStruct((row_count, hidden), jnp.bfloat16),
        scratch_shapes=[
            pltpu.VMEM((part_count, width, hidden), jnp.bfloat16),
            pltpu.VMEM((part_count, width, hidden), jnp.bfloat16),
            pltpu.SemaphoreType.DMA((part_count,)),
            pltpu.SemaphoreType.DMA((part_count,)),
        ],
        compiler_params=pltpu.CompilerParams(vmem_limit_bytes=24 * MIB),
        cost_estimate=SHORT,
        name="hidden_units",
    )(index, *parts, *gains, split, gate_w, up_w)


def columns_kernel(array_count, *refs):
    act_refs, down_ref, out_refs = refs[:array_count], refs[array_count], refs[array_count + 1 :]
    total = None
    source = 0
    for acts in act_refs:
        for i in range(acts.shape[0]):
            part = jnp.dot(acts[i], down_ref[source], preferred_element_type=jnp.float32)
            total = part if source == 0 else total + part
            source += 1
    at = 0
    for out in out_refs:
        rows = out.shape[0]
        out[...] = total[at : at + rows].astype(jnp.bfloat16)
        at += rows


def columns(acts, down_w, piece_rows):
    row_count = acts[0].shape[1]
    width = down_w.shape[2]
    vmem = pl.BlockSpec(memory_space=pltpu.VMEM)
    count = row_count // piece_rows
    return pl.pallas_call(
        functools.partial(columns_kernel, len(acts)),
        in_specs=[vmem] * (len(acts) + 1),
        out_specs=[vmem] * count,
        out_shape=[jax.ShapeDtypeStruct((piece_rows, width), jnp.bfloat16)] * count,
        compiler_params=pltpu.CompilerParams(vmem_limit_bytes=24 * MIB),
        cost_estimate=SHORT,
        name="columns",
    )(*acts, down_w)


def make_stats(stream, gain, router):
    scaled = (stream * gain).astype(jnp.bfloat16)
    logits = lax.dot_general(router, scaled, NT, preferred_element_type=jnp.float32)
    squares = stream * stream
    high = squares.astype(jnp.bfloat16)
    low = (squares - high.astype(jnp.float32)).astype(jnp.bfloat16)
    ones = jnp.ones((8, stream.shape[1]), jnp.bfloat16)
    square = lax.dot_general(ones, high, NT, preferred_element_type=jnp.float32) + lax.dot_general(
        ones, low, NT, preferred_element_type=jnp.float32
    )
    return logits, square


def fill_slots(picks, rows, slot_refs):
    gathered = jnp.dot(picks, rows, preferred_element_type=jnp.float32)
    capacity = slot_refs[0].shape[0]
    for k, out in enumerate(slot_refs):
        out[...] = gathered[k * capacity : (k + 1) * capacity].astype(jnp.bfloat16)


def enter_kernel(expert_count, me_ref, routes_ref, tokens_ref, gain_ref, router_ref, *refs):
    picks_ref, stats_ref = refs[:2]
    slot_refs = refs[2:]
    token_count = tokens_ref.shape[0]
    capacity = slot_refs[0].shape[0]
    relative = lax.broadcasted_iota(jnp.int32, (expert_count, token_count), 0) ^ me_ref[0]
    first, second = routes_ref[0:1, :], routes_ref[1:2, :]
    member = ((relative == first) | (relative == second)).astype(jnp.float32)
    before = lax.broadcasted_iota(jnp.int32, (token_count, token_count), 0)
    after = lax.broadcasted_iota(jnp.int32, (token_count, token_count), 1)
    earlier = (before < after).astype(jnp.bfloat16)
    ranks = jnp.dot(member.astype(jnp.bfloat16), earlier, preferred_element_type=jnp.float32)
    position = lax.broadcasted_iota(jnp.int32, (capacity, token_count), 0).astype(jnp.float32)
    pieces = [
        jnp.where(position == ranks[k : k + 1, :], member[k : k + 1, :], 0.0)
        for k in range(expert_count)
    ]
    picks = jnp.concatenate(pieces, axis=0).astype(jnp.bfloat16)
    picks_ref[...] = picks
    tokens = tokens_ref[...]
    fill_slots(picks, tokens, slot_refs)
    logits, square = make_stats(tokens.astype(jnp.float32), gain_ref[...], router_ref[...])
    stats_ref[0:expert_count, :] = logits
    stats_ref[expert_count:, :] = square


def enter(me, routes, tokens, gain, router, capacity):
    token_count, width = tokens.shape
    expert_count = router.shape[0]
    vmem = pl.BlockSpec(memory_space=pltpu.VMEM)
    return pl.pallas_call(
        functools.partial(enter_kernel, expert_count),
        in_specs=[pl.BlockSpec(memory_space=pltpu.SMEM)] + [vmem] * 4,
        out_shape=[
            jax.ShapeDtypeStruct((expert_count * capacity, token_count), jnp.bfloat16),
            jax.ShapeDtypeStruct((expert_count + 8, token_count), jnp.float32),
        ]
        + [jax.ShapeDtypeStruct((capacity, width), jnp.bfloat16)] * expert_count,
        compiler_params=pltpu.CompilerParams(vmem_limit_bytes=32 * MIB),
        cost_estimate=SHORT,
        name="enter",
    )(me, routes, tokens, gain, router)


def combine_kernel(expert_count, piece_count, full_width, last, me_ref, *refs):
    routes_ref, picks_ref, stats_ref, stream_ref = refs[:4]
    piece_refs = refs[4 : 4 + piece_count]
    rest = refs[4 + piece_count :]
    token_count = stream_ref.shape[0]
    capacity = picks_ref.shape[0] // expert_count
    first, second = routes_ref[0:1, :], routes_ref[1:2, :]
    logits = stats_ref[0:expert_count, :]
    scale = lax.rsqrt(stats_ref[expert_count : expert_count + 1, :] / full_width + 1e-05)
    expert = lax.broadcasted_iota(jnp.int32, (expert_count, token_count), 0)
    first_logit = jnp.sum(jnp.where(expert == first, logits, 0.0), axis=0, keepdims=True)
    second_logit = jnp.sum(jnp.where(expert == second, logits, 0.0), axis=0, keepdims=True)
    first_weight = 1.0 / (1.0 + jnp.exp((second_logit - first_logit) * scale))
    second_weight = 1.0 - first_weight
    relative = expert ^ me_ref[0]
    weight = jnp.where(relative == first, first_weight, 0.0) + jnp.where(
        relative == second, second_weight, 0.0
    )
    picks = picks_ref[...]
    wide_picks = picks.astype(jnp.float32)
    weighted = jnp.concatenate(
        [
            wide_picks[k * capacity : (k + 1) * capacity] * weight[k : k + 1, :]
            for k in range(expert_count)
        ],
        axis=0,
    )
    high = weighted.astype(jnp.bfloat16)
    low = (weighted - high.astype(jnp.float32)).astype(jnp.bfloat16)
    outs = [piece[...] for piece in piece_refs]
    outs = outs[0] if len(outs) == 1 else jnp.concatenate(outs, axis=0)
    added = lax.dot_general(high, outs, TN, preferred_element_type=jnp.float32)
    added = added + lax.dot_general(low, outs, TN, preferred_element_type=jnp.float32)
    stream = stream_ref[...].astype(jnp.float32) + added
    if last:
        rest[0][...] = stream.astype(jnp.bfloat16)
        return
    gain_ref, router_ref, next_ref, next_stats_ref = rest[:4]
    next_ref[...] = stream
    fill_slots(picks, stream.astype(jnp.bfloat16), rest[4:])
    logits, square = make_stats(stream, gain_ref[...], router_ref[...])
    next_stats_ref[0:expert_count, :] = logits
    next_stats_ref[expert_count:, :] = square


def combine(me, routes, picks, stats, stream, pieces, full_width, following):
    token_count, width = stream.shape
    expert_count = stats.shape[0] - 8
    capacity = picks.shape[0] // expert_count
    if capacity % 16:
        pieces = [jnp.concatenate(pieces, axis=0)]
    vmem = pl.BlockSpec(memory_space=pltpu.VMEM)
    operands = [routes, picks, stats, stream, *pieces]
    if following is None:
        out_shape = [jax.ShapeDtypeStruct((token_count, width), jnp.bfloat16)]
    else:
        operands += following
        out_shape = [
            jax.ShapeDtypeStruct((token_count, width), jnp.float32),
            jax.ShapeDtypeStruct(stats.shape, jnp.float32),
        ] + [jax.ShapeDtypeStruct((capacity, width), jnp.bfloat16)] * expert_count
    return pl.pallas_call(
        functools.partial(
            combine_kernel, expert_count, len(pieces), full_width, following is None
        ),
        in_specs=[pl.BlockSpec(memory_space=pltpu.SMEM)] + [vmem] * len(operands),
        out_shape=out_shape,
        compiler_params=pltpu.CompilerParams(vmem_limit_bytes=32 * MIB),
        cost_estimate=SHORT,
        name="combine",
    )(me, *operands)


def ordered(value, *earlier):
    return lax.optimization_barrier((value, earlier))[0]


def gather_parts(parts, bits):
    parts = dict(parts)
    for bit in bits:
        for j in sorted(parts):
            parts[j ^ 1 << bit] = exchange(parts[j], "tensor", 1 << bit)
    return parts


def per_device(
    tokens,
    routes,
    norm_gain,
    router_weight,
    gate_codes,
    gate_scales,
    up_codes,
    up_scales,
    down_codes,
    down_scales,
):
    part_count = lax.axis_size("tensor")
    expert_count = lax.axis_size("expert")
    bits = part_count.bit_length() - 1
    token_count, width = tokens.shape
    full_width = width * part_count
    hidden = gate_codes.shape[3]
    capacity = 3 * token_count // expert_count
    me = lax.axis_index("expert").astype(jnp.int32).reshape(1)
    index = lax.axis_index("tensor").astype(jnp.int32).reshape(1)
    table = jnp.asarray(block_table(), jnp.bfloat16)
    split = jnp.asarray(split_table(hidden), jnp.bfloat16)
    routes_rows = routes.T
    router_rows = jnp.swapaxes(router_weight, 1, 2)

    picks, stats, *slots = enter(
        me, routes_rows, tokens, norm_gain[0:1], router_rows[0], capacity
    )
    first_bits, core_bits = list(reversed(range(1, bits))), [0]
    stream = tokens

    def cores_added(outs):
        kept, away = outs
        return [(kept, 1), (exchange(away, "tensor", 1), 1)]

    def leaving_of(terms):
        total = sum(array[step :: 2 * step].astype(jnp.float32) for array, step in terms)
        return total.astype(jnp.bfloat16)

    def rest_added(terms, leaving):
        for bit in range(1, bits):
            if bit > 1:
                leaving = leaving_of(terms)
            terms = [(array, 2 * step) for array, step in terms]
            terms.append((exchange(leaving, "tensor", 1 << bit), 1))
        return [array for array, _ in terms]

    def give_back(terms, chunk, returned):
        pieces = add_split(terms, capacity)
        for k, piece in zip(chunk, pieces):
            returned[k] = piece if k == 0 else exchange(piece, "expert", k)
        return pieces

    word_rows = down_codes.shape[2]
    scale_rows = down_scales.shape[2]

    def word_block(layer_idx, j):
        at = (index[0] ^ j) * width
        words = lax.dynamic_slice_in_dim(down_codes[layer_idx, 0], at, width, 1)
        scales = lax.dynamic_slice_in_dim(down_scales[layer_idx, 0], at, width, 1)
        spare = jnp.zeros((8 - scale_rows % 8, width), jnp.int32)
        return jnp.concatenate([words, scales, spare], axis=0)

    top = 1 << bits - 1
    moved = {}

    def swap_first(part, wait):
        going = [j for j in range(part_count) if j & top]
        going = going[part * len(going) // 2 : (part + 1) * len(going) // 2]
        payload = wait(jnp.stack([word_block(LAYERS - 1, j) for j in going]))
        arrived = exchange(payload, "tensor", top)
        for i, j in enumerate(going):
            moved[j ^ top] = [(0, word_block(LAYERS - 1, j ^ top)), (top, arrived[i])]
        return payload

    def swap_rest(wait):
        held, payload = dict(moved), None
        for bit in reversed(range(bits - 1)):
            going = [(j, *item) for j in sorted(held) if j >> bit & 1 for item in held[j]]
            payload = wait(jnp.stack([block for _, _, block in going]))
            arrived = exchange(payload, "tensor", 1 << bit)
            held = {j: list(items) for j, items in held.items() if not j >> bit & 1}
            for i, (j, source, _) in enumerate(going):
                held[j ^ 1 << bit].append((source ^ 1 << bit, arrived[i]))
        return payload, [block for _, block in sorted(held[0], key=lambda item: item[0])]

    final = None
    prepared = {}
    whole_gain = None
    for layer_idx in range(LAYERS):
        unit = max(1, expert_count // 8)
        groups = {
            name: [k for u in units for k in range(u * unit, (u + 1) * unit)]
            for name, units in GROUPS[layer_idx]
        }
        arrived = {0: slots[0]}

        def sent(name, slots=slots):
            for k in groups[name]:
                if k not in arrived:
                    arrived[k] = exchange(slots[k], "expert", k)
            return [arrived[k] for k in groups[name]]

        returned = [None] * expert_count
        rows, parts, outs, terms, acts = {}, {}, {}, {}, {}
        by_words = layer_idx == LAYERS - 1
        token = None
        for step, chained in ORDERS[layer_idx]:
            kind, name = step[0], step[1:]

            def wait(value):
                if not chained or token is None:
                    return value
                return ordered(value, token)

            if kind == "R":
                if name not in rows:
                    rows[name] = jnp.concatenate(wait(sent(name)), axis=0)
                else:
                    rows[name] = wait(rows[name])
                parts[name] = gather_parts({0: rows[name]}, first_bits)
                token = rows[name]
            elif kind == "C":
                held = dict(wait(parts[name]))
                token = [held[j] for j in sorted(held) if j > 0]
                held[0] = ordered(held[0], token)
                parts[name] = gather_parts(held, core_bits)
            elif kind == "E" and by_words:
                token = hidden_units(
                    wait(index),
                    [parts[name][j] for j in range(part_count)],
                    [whole_gain[j][layer_idx : layer_idx + 1] for j in range(part_count)],
                    prepared["g", layer_idx],
                    prepared["u", layer_idx],
                    split,
                )
                acts[name] = [token[None], exchange(token, "tensor", 1)[None]]
            elif kind == "X" and by_words:
                for bit in range(1, bits):
                    held = jnp.concatenate(wait(acts[name]), axis=0)
                    token = held
                    acts[name] = [held, exchange(held, "tensor", 1 << bit)]
            elif kind == "P" and by_words:
                token = columns(wait(acts[name]), prepared["d", layer_idx], capacity)
                for k, piece in zip(groups[name], token):
                    returned[k] = piece if k == 0 else exchange(piece, "expert", k)
            elif kind == "V":
                token = swap_first(int(name), wait)
            elif kind == "v":
                token, final = swap_rest(wait)
            elif kind == "E":
                outs[name] = expert_parts(
                    wait(index),
                    [parts[name][j] for j in range(part_count)],
                    [whole_gain[j][layer_idx : layer_idx + 1] for j in range(part_count)],
                    *[prepared[w, layer_idx] for w in "gud"],
                    split,
                )
                token = outs[name]
                terms[name] = cores_added(outs[name])
            elif kind == "X":
                leaving = wait(leaving_of(terms[name]))
                terms[name] = rest_added(terms[name], leaving)
                token = leaving
            elif kind == "P":
                token = give_back(wait(terms[name]), groups[name], returned)
            elif kind == "Z":
                sent(name, wait(slots))
            elif kind == "N":
                rows[name] = jnp.concatenate(wait(sent(name)), axis=0)
                token = rows[name]
            elif kind == "W":
                at = int(name[1:])
                if name[0] == "d" and at == LAYERS - 1:
                    prepared["d", at] = out_weights(wait(final), word_rows)
                elif name[0] == "d":
                    prepared["d", at] = down_rows(down_codes, wait(down_scales), at)
                else:
                    codes, scales = {"g": (gate_codes, gate_scales), "u": (up_codes, up_scales)}[name[0]]
                    prepared[name[0], at] = in_weights(codes, scales, wait(table), at)
                token = prepared[name[0], at]
            elif kind == "S":
                stats = wait(stats)
                for bit in range(bits):
                    stats = stats + exchange(stats, "tensor", 1 << bit)
                token = stats
            elif kind == "G":
                whole_gain = gather_parts({0: wait(norm_gain)}, first_bits + core_bits)
                token = whole_gain
        following = None
        if layer_idx + 1 < LAYERS:
            following = [norm_gain[layer_idx + 1 : layer_idx + 2], router_rows[layer_idx + 1]]
            ready = [value for (_, at), value in prepared.items() if at > layer_idx]
            me = ordered(me, ready)
        results = combine(
            me, routes_rows, picks, stats, stream, returned, full_width, following
        )
        if following is None:
            return results[0]
        stream, stats, *slots = results


def solution(mesh):
    in_specs = (
        P("expert", "tensor"),
        P("expert", None),
        P(None, "tensor"),
        P(None, "tensor", None),
        P(None, "expert", None, "tensor"),
        P(None, "expert", None, "tensor"),
        P(None, "expert", None, "tensor"),
        P(None, "expert", None, "tensor"),
        P(None, "expert", "tensor", None),
        P(None, "expert", "tensor", None),
    )
    out_specs = P("expert", "tensor")
    return jax.shard_map(
        per_device, mesh=mesh, in_specs=in_specs, out_specs=out_specs, check_vma=False
    )
```

```python
import functools
import math

import jax
import jax.numpy as jnp
import numpy as np
from jax import lax
from jax.experimental import pallas as pl
from jax.experimental.pallas import tpu as pltpu
from jax.sharding import PartitionSpec as P

LAYERS = 2
ORDERS = (
    (
        ("Wg0", 1), ("G", 0), ("S", 0), ("Ra", 1), ("Wu0", 1), ("Wd0", 1), ("Rb", 1),
        ("Ca", 0), ("Cb", 1), ("Ea", 0), ("Xa", 1), ("Eb", 0), ("Xb", 1), ("Pb", 1),
        ("Wd1", 1), ("Wu1", 1), ("Pa", 1), ("Wg1", 1),
    ),
    (
        ("S", 1), ("Ra", 0), ("Rb", 0), ("Ca", 1), ("Ea", 1), ("Cb", 1), ("Eb", 0), ("Xb", 1),
        ("Xa", 1), ("Pb", 1), ("Pa", 0),
    ),
)
GROUPS = (
    ("a", (0, 1, 2, 3)),
    ("b", (4, 5, 6, 7)),
)
GROUP = 128
BLOCK = 256
MIB = 1 << 20
FIRST = 8
SECOND = 64
NT = (((1,), (1,)), ((), ()))
TN = (((0,), (0,)), ((), ()))


def exchange(shard, axis, mask):
    return lax.ppermute(shard, axis, [(i, i ^ mask) for i in range(lax.axis_size(axis))])


def block_table():
    index = np.arange(BLOCK)
    order = np.concatenate([index[0::2], index[1::2]])
    common = index[:, None] & order[None, :]
    ones = np.array([bin(v).count("1") for v in range(BLOCK)])[common]
    return np.where(ones % 2 == 1, -1.0, 1.0).astype(np.float32)


def split_table(width):
    table = np.zeros((width, width), np.float32)
    for unit in range(width):
        table[unit, unit % 2 * (width // 2) + unit // 2] = 1.0
    return table


def power(exponents):
    return (1 << (16 - exponents)).astype(jnp.float32) * (1.0 / 65536.0)


SHORT = pl.CostEstimate(flops=1000, bytes_accessed=1000, transcendentals=0)


def butterfly(rows, start):
    stride = start
    while stride < len(rows):
        for b in range(len(rows)):
            if b & stride == 0:
                low, high = rows[b], rows[b + stride]
                rows[b], rows[b + stride] = low + high, low - high
        stride *= 2


def in_weights_kernel(first_steps, words_ref, scales_ref, table_ref, out_ref, sums_ref):
    half = BLOCK // 2
    words_group = GROUP // 2
    groups_block = BLOCK // GROUP
    step = pl.program_id(0)
    width = words_ref.shape[3]
    block_count = out_ref.shape[0]

    @pl.when(step < first_steps)
    def _():
        sums = []
        for q in range(FIRST):
            words = words_ref[0, 0, q * half : (q + 1) * half, :]
            pieces = []
            for shift in (0, 4):
                codes = ((words >> shift) & 15).astype(jnp.float32) - 8.0
                for g in range(groups_block):
                    at = q * groups_block + g
                    factor = power(scales_ref[0, 0, at : at + 1, :])
                    pieces.append(codes[g * words_group : (g + 1) * words_group] * factor)
            block = jnp.concatenate(pieces, axis=0).astype(jnp.bfloat16)
            sums.append(jnp.dot(table_ref[...], block, preferred_element_type=jnp.float32))
        butterfly(sums, 1)
        for q in range(FIRST):
            sums_ref[step * FIRST + q] = sums[q]

    @pl.when(step >= first_steps)
    def _():
        base = (step - first_steps) * SECOND
        for r in range(0, SECOND, 16):
            for c in range(0, width, 128):
                for q in range(FIRST):
                    rows = [
                        sums_ref[b * FIRST + q, pl.ds(pl.multiple_of(base + r, 16), 16), c : c + 128]
                        for b in range(block_count // FIRST)
                    ]
                    butterfly(rows, 1)
                    for b, row in enumerate(rows):
                        out_ref[b * FIRST + q, r : r + 16, c : c + 128] = row.astype(jnp.bfloat16)


def in_weights(words, scales, table, layer_idx):
    _, _, word_rows, width = words.shape
    full = 2 * word_rows
    block_count = full // BLOCK
    first_steps = block_count // FIRST
    word_tile = FIRST * BLOCK // 2
    group_tile = FIRST * BLOCK // GROUP
    out = pl.pallas_call(
        functools.partial(in_weights_kernel, first_steps),
        grid=(first_steps + BLOCK // SECOND,),
        in_specs=[
            pl.BlockSpec(
                (1, 1, word_tile, width),
                lambda i: (layer_idx, 0, jnp.minimum(i, first_steps - 1), 0),
            ),
            pl.BlockSpec(
                (1, 1, group_tile, width),
                lambda i: (layer_idx, 0, jnp.minimum(i, first_steps - 1), 0),
            ),
            pl.BlockSpec((BLOCK, BLOCK), lambda i: (0, 0)),
        ],
        out_specs=pl.BlockSpec(
            (block_count, SECOND, width), lambda i: (0, jnp.maximum(i - first_steps, 0), 0)
        ),
        out_shape=jax.ShapeDtypeStruct((block_count, BLOCK, width), jnp.bfloat16),
        scratch_shapes=[pltpu.VMEM((block_count, BLOCK, width), jnp.float32)],
        compiler_params=pltpu.CompilerParams(vmem_limit_bytes=54 * MIB),
        cost_estimate=SHORT,
        name="in_weights",
    )(words, scales, table)
    return out.reshape(full, width)


def out_weights_kernel(words_ref, scales_ref, out_ref):
    words = words_ref[0, 0]
    word_rows = words.shape[0]
    words_group = GROUP // 2
    for part, shift in enumerate((0, 4)):
        codes = ((words >> shift) & 15).astype(jnp.float32) - 8.0
        for g in range(word_rows // words_group):
            factor = power(scales_ref[0, 0, pl.ds(g, 1), :])
            out_ref[pl.ds(part * word_rows + g * words_group, words_group), :] = (
                codes[g * words_group : (g + 1) * words_group] * factor
            ).astype(jnp.bfloat16)


def out_weights(words, scales, layer_idx):
    _, _, word_rows, width = words.shape
    groups = scales.shape[2]
    tile = width // 2
    return pl.pallas_call(
        out_weights_kernel,
        grid=(width // tile,),
        in_specs=[
            pl.BlockSpec((1, 1, word_rows, tile), lambda c: (layer_idx, 0, 0, c)),
            pl.BlockSpec((1, 1, groups, tile), lambda c: (layer_idx, 0, 0, c)),
        ],
        out_specs=pl.BlockSpec((2 * word_rows, tile), lambda c: (0, c)),
        out_shape=jax.ShapeDtypeStruct((2 * word_rows, width), jnp.bfloat16),
        compiler_params=pltpu.CompilerParams(vmem_limit_bytes=54 * MIB),
        cost_estimate=SHORT,
        name="out_weights",
    )(words, scales)


def expert_kernel(part_count, full_width, index_ref, *refs):
    x_refs, refs = refs[:part_count], refs[part_count:]
    gain_refs, refs = refs[:part_count], refs[part_count:]
    split_ref, gate_hbm, up_hbm, down_hbm = refs[:4]
    out_refs, refs = refs[4:6], refs[6:]
    gate_ref, up_ref, down_ref, gate_sem, up_sem, down_sem = refs
    width = x_refs[0].shape[1]
    copies = [[], [], []]
    for j in range(part_count):
        at = pl.ds(pl.multiple_of((index_ref[0] ^ j) * width, width), width)
        copies[0].append(
            pltpu.make_async_copy(gate_hbm.at[at, :], gate_ref.at[j], gate_sem.at[j])
        )
        copies[1].append(pltpu.make_async_copy(up_hbm.at[at, :], up_ref.at[j], up_sem.at[j]))
        copies[2].append(
            pltpu.make_async_copy(down_hbm.at[:, at], down_ref.at[j], down_sem.at[j])
        )
    for j in range(part_count):
        copies[0][j].start()
        copies[1][j].start()
    for j in range(part_count):
        copies[2][j].start()
    gate = up = square = None
    for j in range(part_count):
        wide = x_refs[j][...].astype(jnp.float32)
        rows = (wide * gain_refs[j][...]).astype(jnp.bfloat16)
        part = jnp.sum(wide * wide, axis=1, keepdims=True)
        square = part if j == 0 else square + part
        copies[0][j].wait()
        part = jnp.dot(rows, gate_ref[j], preferred_element_type=jnp.float32)
        gate = part if j == 0 else gate + part
        copies[1][j].wait()
        part = jnp.dot(rows, up_ref[j], preferred_element_type=jnp.float32)
        up = part if j == 0 else up + part
    scale = lax.rsqrt(square / full_width + 1e-05) * (1.0 / math.sqrt(full_width))
    gate = gate * scale
    act = (gate / (1.0 + jnp.exp(-gate))) * (up * scale)
    act = jnp.dot(
        act.astype(jnp.bfloat16), split_ref[...], preferred_element_type=jnp.float32
    ).astype(jnp.bfloat16)
    for j in range(part_count):
        copies[2][j].wait()
        out_refs[j % 2][j // 2] = jnp.dot(
            act, down_ref[j], preferred_element_type=jnp.float32
        ).astype(jnp.bfloat16)


def expert_parts(index, parts, gains, gate_w, up_w, down_w, split):
    part_count = len(parts)
    row_count, width = parts[0].shape
    full_width, hidden = gate_w.shape
    vmem = pl.BlockSpec(memory_space=pltpu.VMEM)
    hbm = pl.BlockSpec(memory_space=pltpu.HBM)
    return pl.pallas_call(
        functools.partial(expert_kernel, part_count, full_width),
        in_specs=[pl.BlockSpec(memory_space=pltpu.SMEM)]
        + [vmem] * (2 * part_count + 1)
        + [hbm] * 3,
        out_specs=[vmem] * 2,
        out_shape=[jax.ShapeDtypeStruct((part_count // 2, row_count, width), jnp.bfloat16)] * 2,
        scratch_shapes=[
            pltpu.VMEM((part_count, width, hidden), jnp.bfloat16),
            pltpu.VMEM((part_count, width, hidden), jnp.bfloat16),
            pltpu.VMEM((part_count, hidden, width), jnp.bfloat16),
            pltpu.SemaphoreType.DMA((part_count,)),
            pltpu.SemaphoreType.DMA((part_count,)),
            pltpu.SemaphoreType.DMA((part_count,)),
        ],
        compiler_params=pltpu.CompilerParams(vmem_limit_bytes=36 * MIB),
        cost_estimate=SHORT,
        name="expert_parts",
    )(index, *parts, *gains, split, gate_w, up_w, down_w)


def add_split_kernel(term_count, *refs):
    total = refs[0][0].astype(jnp.float32)
    for term in refs[1:term_count]:
        total = total + term[0].astype(jnp.float32)
    at = 0
    for out in refs[term_count:]:
        rows = out.shape[0]
        out[...] = total[at : at + rows].astype(jnp.bfloat16)
        at += rows


def add_split(terms, piece_rows):
    _, row_count, width = terms[0].shape
    vmem = pl.BlockSpec(memory_space=pltpu.VMEM)
    count = row_count // piece_rows
    return pl.pallas_call(
        functools.partial(add_split_kernel, len(terms)),
        in_specs=[vmem] * len(terms),
        out_specs=[vmem] * count,
        out_shape=[jax.ShapeDtypeStruct((piece_rows, width), jnp.bfloat16)] * count,
        compiler_params=pltpu.CompilerParams(vmem_limit_bytes=32 * MIB),
        cost_estimate=SHORT,
        name="add_split",
    )(*terms)


def make_stats(stream, gain, router):
    scaled = (stream * gain).astype(jnp.bfloat16)
    logits = lax.dot_general(router, scaled, NT, preferred_element_type=jnp.float32)
    squares = stream * stream
    high = squares.astype(jnp.bfloat16)
    low = (squares - high.astype(jnp.float32)).astype(jnp.bfloat16)
    ones = jnp.ones((8, stream.shape[1]), jnp.bfloat16)
    square = lax.dot_general(ones, high, NT, preferred_element_type=jnp.float32) + lax.dot_general(
        ones, low, NT, preferred_element_type=jnp.float32
    )
    return logits, square


def fill_slots(picks, rows, slot_refs):
    gathered = jnp.dot(picks, rows, preferred_element_type=jnp.float32)
    capacity = slot_refs[0].shape[0]
    for k, out in enumerate(slot_refs):
        out[...] = gathered[k * capacity : (k + 1) * capacity].astype(jnp.bfloat16)


def enter_kernel(expert_count, me_ref, routes_ref, tokens_ref, gain_ref, router_ref, *refs):
    picks_ref, stats_ref = refs[:2]
    slot_refs = refs[2:]
    token_count = tokens_ref.shape[0]
    capacity = slot_refs[0].shape[0]
    relative = lax.broadcasted_iota(jnp.int32, (expert_count, token_count), 0) ^ me_ref[0]
    first, second = routes_ref[0:1, :], routes_ref[1:2, :]
    member = ((relative == first) | (relative == second)).astype(jnp.float32)
    before = lax.broadcasted_iota(jnp.int32, (token_count, token_count), 0)
    after = lax.broadcasted_iota(jnp.int32, (token_count, token_count), 1)
    earlier = (before < after).astype(jnp.bfloat16)
    ranks = jnp.dot(member.astype(jnp.bfloat16), earlier, preferred_element_type=jnp.float32)
    position = lax.broadcasted_iota(jnp.int32, (capacity, token_count), 0).astype(jnp.float32)
    pieces = [
        jnp.where(position == ranks[k : k + 1, :], member[k : k + 1, :], 0.0)
        for k in range(expert_count)
    ]
    picks = jnp.concatenate(pieces, axis=0).astype(jnp.bfloat16)
    picks_ref[...] = picks
    tokens = tokens_ref[...]
    fill_slots(picks, tokens, slot_refs)
    logits, square = make_stats(tokens.astype(jnp.float32), gain_ref[...], router_ref[...])
    stats_ref[0:expert_count, :] = logits
    stats_ref[expert_count:, :] = square


def enter(me, routes, tokens, gain, router, capacity):
    token_count, width = tokens.shape
    expert_count = router.shape[0]
    vmem = pl.BlockSpec(memory_space=pltpu.VMEM)
    return pl.pallas_call(
        functools.partial(enter_kernel, expert_count),
        in_specs=[pl.BlockSpec(memory_space=pltpu.SMEM)] + [vmem] * 4,
        out_shape=[
            jax.ShapeDtypeStruct((expert_count * capacity, token_count), jnp.bfloat16),
            jax.ShapeDtypeStruct((expert_count + 8, token_count), jnp.float32),
        ]
        + [jax.ShapeDtypeStruct((capacity, width), jnp.bfloat16)] * expert_count,
        compiler_params=pltpu.CompilerParams(vmem_limit_bytes=32 * MIB),
        cost_estimate=SHORT,
        name="enter",
    )(me, routes, tokens, gain, router)


def combine_kernel(expert_count, piece_count, full_width, last, me_ref, *refs):
    routes_ref, picks_ref, stats_ref, stream_ref = refs[:4]
    piece_refs = refs[4 : 4 + piece_count]
    rest = refs[4 + piece_count :]
    token_count = stream_ref.shape[0]
    capacity = picks_ref.shape[0] // expert_count
    first, second = routes_ref[0:1, :], routes_ref[1:2, :]
    logits = stats_ref[0:expert_count, :]
    scale = lax.rsqrt(stats_ref[expert_count : expert_count + 1, :] / full_width + 1e-05)
    expert = lax.broadcasted_iota(jnp.int32, (expert_count, token_count), 0)
    first_logit = jnp.sum(jnp.where(expert == first, logits, 0.0), axis=0, keepdims=True)
    second_logit = jnp.sum(jnp.where(expert == second, logits, 0.0), axis=0, keepdims=True)
    first_weight = 1.0 / (1.0 + jnp.exp((second_logit - first_logit) * scale))
    second_weight = 1.0 - first_weight
    relative = expert ^ me_ref[0]
    weight = jnp.where(relative == first, first_weight, 0.0) + jnp.where(
        relative == second, second_weight, 0.0
    )
    picks = picks_ref[...]
    wide_picks = picks.astype(jnp.float32)
    weighted = jnp.concatenate(
        [
            wide_picks[k * capacity : (k + 1) * capacity] * weight[k : k + 1, :]
            for k in range(expert_count)
        ],
        axis=0,
    )
    high = weighted.astype(jnp.bfloat16)
    low = (weighted - high.astype(jnp.float32)).astype(jnp.bfloat16)
    outs = [piece[...] for piece in piece_refs]
    outs = outs[0] if len(outs) == 1 else jnp.concatenate(outs, axis=0)
    added = lax.dot_general(high, outs, TN, preferred_element_type=jnp.float32)
    added = added + lax.dot_general(low, outs, TN, preferred_element_type=jnp.float32)
    stream = stream_ref[...].astype(jnp.float32) + added
    if last:
        rest[0][...] = stream.astype(jnp.bfloat16)
        return
    gain_ref, router_ref, next_ref, next_stats_ref = rest[:4]
    next_ref[...] = stream
    fill_slots(picks, stream.astype(jnp.bfloat16), rest[4:])
    logits, square = make_stats(stream, gain_ref[...], router_ref[...])
    next_stats_ref[0:expert_count, :] = logits
    next_stats_ref[expert_count:, :] = square


def combine(me, routes, picks, stats, stream, pieces, full_width, following):
    token_count, width = stream.shape
    expert_count = stats.shape[0] - 8
    capacity = picks.shape[0] // expert_count
    if capacity % 16:
        pieces = [jnp.concatenate(pieces, axis=0)]
    vmem = pl.BlockSpec(memory_space=pltpu.VMEM)
    operands = [routes, picks, stats, stream, *pieces]
    if following is None:
        out_shape = [jax.ShapeDtypeStruct((token_count, width), jnp.bfloat16)]
    else:
        operands += following
        out_shape = [
            jax.ShapeDtypeStruct((token_count, width), jnp.float32),
            jax.ShapeDtypeStruct(stats.shape, jnp.float32),
        ] + [jax.ShapeDtypeStruct((capacity, width), jnp.bfloat16)] * expert_count
    return pl.pallas_call(
        functools.partial(
            combine_kernel, expert_count, len(pieces), full_width, following is None
        ),
        in_specs=[pl.BlockSpec(memory_space=pltpu.SMEM)] + [vmem] * len(operands),
        out_shape=out_shape,
        compiler_params=pltpu.CompilerParams(vmem_limit_bytes=32 * MIB),
        cost_estimate=SHORT,
        name="combine",
    )(me, *operands)


def ordered(value, *earlier):
    return lax.optimization_barrier((value, earlier))[0]


def gather_parts(parts, bits):
    parts = dict(parts)
    for bit in bits:
        for j in sorted(parts):
            parts[j ^ 1 << bit] = exchange(parts[j], "tensor", 1 << bit)
    return parts


def per_device(
    tokens,
    routes,
    norm_gain,
    router_weight,
    gate_codes,
    gate_scales,
    up_codes,
    up_scales,
    down_codes,
    down_scales,
):
    part_count = lax.axis_size("tensor")
    expert_count = lax.axis_size("expert")
    bits = part_count.bit_length() - 1
    token_count, width = tokens.shape
    full_width = width * part_count
    hidden = gate_codes.shape[3]
    capacity = 3 * token_count // expert_count
    me = lax.axis_index("expert").astype(jnp.int32).reshape(1)
    index = lax.axis_index("tensor").astype(jnp.int32).reshape(1)
    table = jnp.asarray(block_table(), jnp.bfloat16)
    split = jnp.asarray(split_table(hidden), jnp.bfloat16)
    routes_rows = routes.T
    router_rows = jnp.swapaxes(router_weight, 1, 2)

    picks, stats, *slots = enter(
        me, routes_rows, tokens, norm_gain[0:1], router_rows[0], capacity
    )
    first_bits, core_bits = list(reversed(range(1, bits))), [0]
    stream = tokens

    def cores_added(outs):
        kept, away = outs
        return [(kept, 1), (exchange(away, "tensor", 1), 1)]

    def leaving_of(terms):
        total = sum(array[step :: 2 * step].astype(jnp.float32) for array, step in terms)
        return total.astype(jnp.bfloat16)

    def rest_added(terms, leaving):
        for bit in range(1, bits):
            if bit > 1:
                leaving = leaving_of(terms)
            terms = [(array, 2 * step) for array, step in terms]
            terms.append((exchange(leaving, "tensor", 1 << bit), 1))
        return [array for array, _ in terms]

    def give_back(terms, chunk, returned):
        pieces = add_split(terms, capacity)
        for k, piece in zip(chunk, pieces):
            returned[k] = piece if k == 0 else exchange(piece, "expert", k)
        return pieces

    unit = max(1, expert_count // 8)
    groups = {
        name: [k for u in units for k in range(u * unit, (u + 1) * unit)]
        for name, units in GROUPS
    }
    prepared = {}
    whole_gain = None
    for layer_idx in range(LAYERS):
        arrived = {0: slots[0]}

        def sent(name, slots=slots):
            for k in groups[name]:
                if k not in arrived:
                    arrived[k] = exchange(slots[k], "expert", k)
            return [arrived[k] for k in groups[name]]

        returned = [None] * expert_count
        rows, parts, outs, terms = {}, {}, {}, {}
        token = None
        for step, chained in ORDERS[layer_idx]:
            kind, name = step[0], step[1:]

            def wait(value):
                if not chained or token is None:
                    return value
                return ordered(value, token)

            if kind == "R":
                if name not in rows:
                    rows[name] = jnp.concatenate(wait(sent(name)), axis=0)
                else:
                    rows[name] = wait(rows[name])
                parts[name] = gather_parts({0: rows[name]}, first_bits)
                token = rows[name]
            elif kind == "C":
                held = dict(wait(parts[name]))
                token = [held[j] for j in sorted(held) if j > 0]
                held[0] = ordered(held[0], token)
                parts[name] = gather_parts(held, core_bits)
            elif kind == "E":
                outs[name] = expert_parts(
                    wait(index),
                    [parts[name][j] for j in range(part_count)],
                    [whole_gain[j][layer_idx : layer_idx + 1] for j in range(part_count)],
                    *[prepared[w, layer_idx] for w in "gud"],
                    split,
                )
                token = outs[name]
                terms[name] = cores_added(outs[name])
            elif kind == "X":
                leaving = wait(leaving_of(terms[name]))
                terms[name] = rest_added(terms[name], leaving)
                token = leaving
            elif kind == "P":
                token = give_back(wait(terms[name]), groups[name], returned)
            elif kind == "Z":
                sent(name, wait(slots))
            elif kind == "N":
                rows[name] = jnp.concatenate(wait(sent(name)), axis=0)
                token = rows[name]
            elif kind == "W":
                at = int(name[1:])
                if name[0] == "d":
                    prepared["d", at] = out_weights(down_codes, wait(down_scales), at)
                else:
                    codes, scales = {"g": (gate_codes, gate_scales), "u": (up_codes, up_scales)}[name[0]]
                    prepared[name[0], at] = in_weights(codes, scales, wait(table), at)
                token = prepared[name[0], at]
            elif kind == "S":
                stats = wait(stats)
                for bit in range(bits):
                    stats = stats + exchange(stats, "tensor", 1 << bit)
                token = stats
            elif kind == "G":
                whole_gain = gather_parts({0: wait(norm_gain)}, first_bits + core_bits)
                token = whole_gain
        following = None
        if layer_idx + 1 < LAYERS:
            following = [norm_gain[layer_idx + 1 : layer_idx + 2], router_rows[layer_idx + 1]]
            ready = [value for (_, at), value in prepared.items() if at > layer_idx]
            if ready:
                me = ordered(me, ready)
        results = combine(
            me, routes_rows, picks, stats, stream, returned, full_width, following
        )
        if following is None:
            return results[0]
        stream, stats, *slots = results


def solution(mesh):
    in_specs = (
        P("expert", "tensor"),
        P("expert", None),
        P(None, "tensor"),
        P(None, "tensor", None),
        P(None, "expert", None, "tensor"),
        P(None, "expert", None, "tensor"),
        P(None, "expert", None, "tensor"),
        P(None, "expert", None, "tensor"),
        P(None, "expert", "tensor", None),
        P(None, "expert", "tensor", None),
    )
    out_specs = P("expert", "tensor")
    return jax.shard_map(
        per_device, mesh=mesh, in_specs=in_specs, out_specs=out_specs, check_vma=False
    )
```

```python
import functools
import math

import jax
import jax.numpy as jnp
import numpy as np
from jax import lax
from jax.experimental import pallas as pl
from jax.experimental.pallas import tpu as pltpu
from jax.sharding import PartitionSpec as P

LAYERS = 2
ORDERS = (
    (
        ("S", 0), ("Ra", 1), ("Wg0", 1), ("Wd0", 1), ("Wu0", 1), ("Rb", 1), ("Ca", 0),
        ("Ea", 0), ("Cb", 1), ("Xa", 0), ("Eb", 0), ("Xb", 1), ("Wg1", 1), ("Pb", 1),
        ("Wu1", 1), ("Pa", 1), ("Wd1", 1),
    ),
    (
        ("S", 1), ("Ra", 0), ("Rb", 0), ("Ca", 1), ("Ea", 1), ("Cb", 1), ("Eb", 1), ("Xb", 1),
        ("Xa", 0), ("Pb", 1), ("Pa", 1),
    ),
)
GROUPS = (
    ("a", (0, 1, 2, 3)),
    ("b", (4, 5, 6, 7)),
)
GROUP = 128
BLOCK = 256
MIB = 1 << 20
FIRST = 8
SECOND = 64
NT = (((1,), (1,)), ((), ()))
TN = (((0,), (0,)), ((), ()))


def exchange(shard, axis, mask):
    return lax.ppermute(shard, axis, [(i, i ^ mask) for i in range(lax.axis_size(axis))])


def block_table():
    index = np.arange(BLOCK)
    order = np.concatenate([index[0::2], index[1::2]])
    common = index[:, None] & order[None, :]
    ones = np.array([bin(v).count("1") for v in range(BLOCK)])[common]
    return np.where(ones % 2 == 1, -1.0, 1.0).astype(np.float32)


def split_table(width):
    table = np.zeros((width, width), np.float32)
    for unit in range(width):
        table[unit, unit % 2 * (width // 2) + unit // 2] = 1.0
    return table


def power(exponents):
    return (1 << (16 - exponents)).astype(jnp.float32) * (1.0 / 65536.0)


SHORT = pl.CostEstimate(flops=1000, bytes_accessed=1000, transcendentals=0)


def butterfly(rows, start):
    stride = start
    while stride < len(rows):
        for b in range(len(rows)):
            if b & stride == 0:
                low, high = rows[b], rows[b + stride]
                rows[b], rows[b + stride] = low + high, low - high
        stride *= 2


def in_weights_kernel(first_steps, words_ref, scales_ref, table_ref, out_ref, sums_ref):
    half = BLOCK // 2
    words_group = GROUP // 2
    groups_block = BLOCK // GROUP
    step = pl.program_id(0)
    width = words_ref.shape[3]
    block_count = out_ref.shape[0]

    @pl.when(step < first_steps)
    def _():
        sums = []
        for q in range(FIRST):
            words = words_ref[0, 0, q * half : (q + 1) * half, :]
            pieces = []
            for shift in (0, 4):
                codes = ((words >> shift) & 15).astype(jnp.float32) - 8.0
                for g in range(groups_block):
                    at = q * groups_block + g
                    factor = power(scales_ref[0, 0, at : at + 1, :])
                    pieces.append(codes[g * words_group : (g + 1) * words_group] * factor)
            block = jnp.concatenate(pieces, axis=0).astype(jnp.bfloat16)
            sums.append(jnp.dot(table_ref[...], block, preferred_element_type=jnp.float32))
        butterfly(sums, 1)
        for q in range(FIRST):
            sums_ref[step * FIRST + q] = sums[q]

    @pl.when(step >= first_steps)
    def _():
        base = (step - first_steps) * SECOND
        for r in range(0, SECOND, 16):
            for c in range(0, width, 128):
                for q in range(FIRST):
                    rows = [
                        sums_ref[b * FIRST + q, pl.ds(pl.multiple_of(base + r, 16), 16), c : c + 128]
                        for b in range(block_count // FIRST)
                    ]
                    butterfly(rows, 1)
                    for b, row in enumerate(rows):
                        out_ref[b * FIRST + q, r : r + 16, c : c + 128] = row.astype(jnp.bfloat16)


def in_weights(words, scales, table, layer_idx):
    _, _, word_rows, width = words.shape
    full = 2 * word_rows
    block_count = full // BLOCK
    first_steps = block_count // FIRST
    word_tile = FIRST * BLOCK // 2
    group_tile = FIRST * BLOCK // GROUP
    out = pl.pallas_call(
        functools.partial(in_weights_kernel, first_steps),
        grid=(first_steps + BLOCK // SECOND,),
        in_specs=[
            pl.BlockSpec(
                (1, 1, word_tile, width),
                lambda i: (layer_idx, 0, jnp.minimum(i, first_steps - 1), 0),
            ),
            pl.BlockSpec(
                (1, 1, group_tile, width),
                lambda i: (layer_idx, 0, jnp.minimum(i, first_steps - 1), 0),
            ),
            pl.BlockSpec((BLOCK, BLOCK), lambda i: (0, 0)),
        ],
        out_specs=pl.BlockSpec(
            (block_count, SECOND, width), lambda i: (0, jnp.maximum(i - first_steps, 0), 0)
        ),
        out_shape=jax.ShapeDtypeStruct((block_count, BLOCK, width), jnp.bfloat16),
        scratch_shapes=[pltpu.VMEM((block_count, BLOCK, width), jnp.float32)],
        compiler_params=pltpu.CompilerParams(vmem_limit_bytes=54 * MIB),
        cost_estimate=SHORT,
        name="in_weights",
    )(words, scales, table)
    return out.reshape(full, width)


def out_weights_kernel(words_ref, scales_ref, out_ref):
    words = words_ref[0, 0]
    word_rows = words.shape[0]
    words_group = GROUP // 2
    for part, shift in enumerate((0, 4)):
        codes = ((words >> shift) & 15).astype(jnp.float32) - 8.0
        for g in range(word_rows // words_group):
            factor = power(scales_ref[0, 0, pl.ds(g, 1), :])
            out_ref[pl.ds(part * word_rows + g * words_group, words_group), :] = (
                codes[g * words_group : (g + 1) * words_group] * factor
            ).astype(jnp.bfloat16)


def out_weights(words, scales, layer_idx):
    _, _, word_rows, width = words.shape
    groups = scales.shape[2]
    tile = width // 2
    return pl.pallas_call(
        out_weights_kernel,
        grid=(width // tile,),
        in_specs=[
            pl.BlockSpec((1, 1, word_rows, tile), lambda c: (layer_idx, 0, 0, c)),
            pl.BlockSpec((1, 1, groups, tile), lambda c: (layer_idx, 0, 0, c)),
        ],
        out_specs=pl.BlockSpec((2 * word_rows, tile), lambda c: (0, c)),
        out_shape=jax.ShapeDtypeStruct((2 * word_rows, width), jnp.bfloat16),
        compiler_params=pltpu.CompilerParams(vmem_limit_bytes=54 * MIB),
        cost_estimate=SHORT,
        name="out_weights",
    )(words, scales)


def expert_kernel(part_count, full_width, layer_idx, index_ref, *refs):
    x_refs, refs = refs[:part_count], refs[part_count:]
    gains_ref, split_ref, gate_hbm, up_hbm, down_hbm = refs[:5]
    refs = refs[1:]
    out_refs, refs = refs[4:6], refs[6:]
    gate_ref, up_ref, down_ref, gate_sem, up_sem, down_sem = refs
    width = x_refs[0].shape[1]
    copies = [[], [], []]
    for j in range(part_count):
        at = pl.ds(pl.multiple_of((index_ref[0] ^ j) * width, width), width)
        copies[0].append(
            pltpu.make_async_copy(gate_hbm.at[at, :], gate_ref.at[j], gate_sem.at[j])
        )
        copies[1].append(pltpu.make_async_copy(up_hbm.at[at, :], up_ref.at[j], up_sem.at[j]))
        copies[2].append(
            pltpu.make_async_copy(down_hbm.at[:, at], down_ref.at[j], down_sem.at[j])
        )
    for j in range(part_count):
        copies[0][j].start()
        copies[1][j].start()
    for j in range(part_count):
        copies[2][j].start()
    gate = up = square = None
    for j in range(part_count):
        wide = x_refs[j][...].astype(jnp.float32)
        gain = gains_ref[pl.ds((index_ref[0] ^ j) * LAYERS + layer_idx, 1), :]
        rows = (wide * gain).astype(jnp.bfloat16)
        part = jnp.sum(wide * wide, axis=1, keepdims=True)
        square = part if j == 0 else square + part
        copies[0][j].wait()
        part = jnp.dot(rows, gate_ref[j], preferred_element_type=jnp.float32)
        gate = part if j == 0 else gate + part
        copies[1][j].wait()
        part = jnp.dot(rows, up_ref[j], preferred_element_type=jnp.float32)
        up = part if j == 0 else up + part
    scale = lax.rsqrt(square / full_width + 1e-05) * (1.0 / math.sqrt(full_width))
    gate = gate * scale
    act = (gate / (1.0 + jnp.exp(-gate))) * (up * scale)
    act = jnp.dot(
        act.astype(jnp.bfloat16), split_ref[...], preferred_element_type=jnp.float32
    ).astype(jnp.bfloat16)
    for j in range(part_count):
        copies[2][j].wait()
        out_refs[j % 2][j // 2] = jnp.dot(
            act, down_ref[j], preferred_element_type=jnp.float32
        ).astype(jnp.bfloat16)


def expert_parts(layer_idx, index, parts, gains, gate_w, up_w, down_w, split):
    part_count = len(parts)
    row_count, width = parts[0].shape
    full_width, hidden = gate_w.shape
    vmem = pl.BlockSpec(memory_space=pltpu.VMEM)
    hbm = pl.BlockSpec(memory_space=pltpu.HBM)
    return pl.pallas_call(
        functools.partial(expert_kernel, part_count, full_width, layer_idx),
        in_specs=[pl.BlockSpec(memory_space=pltpu.SMEM)]
        + [vmem] * (part_count + 2)
        + [hbm] * 3,
        out_specs=[vmem] * 2,
        out_shape=[jax.ShapeDtypeStruct((part_count // 2, row_count, width), jnp.bfloat16)] * 2,
        scratch_shapes=[
            pltpu.VMEM((part_count, width, hidden), jnp.bfloat16),
            pltpu.VMEM((part_count, width, hidden), jnp.bfloat16),
            pltpu.VMEM((part_count, hidden, width), jnp.bfloat16),
            pltpu.SemaphoreType.DMA((part_count,)),
            pltpu.SemaphoreType.DMA((part_count,)),
            pltpu.SemaphoreType.DMA((part_count,)),
        ],
        compiler_params=pltpu.CompilerParams(vmem_limit_bytes=36 * MIB),
        cost_estimate=SHORT,
        name="expert_parts",
    )(index, *parts, gains, split, gate_w, up_w, down_w)


def add_split_kernel(term_count, *refs):
    total = refs[0][0].astype(jnp.float32)
    for term in refs[1:term_count]:
        total = total + term[0].astype(jnp.float32)
    at = 0
    for out in refs[term_count:]:
        rows = out.shape[0]
        out[...] = total[at : at + rows].astype(jnp.bfloat16)
        at += rows


def add_split(terms, piece_rows):
    _, row_count, width = terms[0].shape
    vmem = pl.BlockSpec(memory_space=pltpu.VMEM)
    count = row_count // piece_rows
    return pl.pallas_call(
        functools.partial(add_split_kernel, len(terms)),
        in_specs=[vmem] * len(terms),
        out_specs=[vmem] * count,
        out_shape=[jax.ShapeDtypeStruct((piece_rows, width), jnp.bfloat16)] * count,
        compiler_params=pltpu.CompilerParams(vmem_limit_bytes=32 * MIB),
        cost_estimate=SHORT,
        name="add_split",
    )(*terms)


def make_stats(stream, gain, router):
    scaled = (stream * gain).astype(jnp.bfloat16)
    logits = lax.dot_general(router, scaled, NT, preferred_element_type=jnp.float32)
    squares = stream * stream
    high = squares.astype(jnp.bfloat16)
    low = (squares - high.astype(jnp.float32)).astype(jnp.bfloat16)
    ones = jnp.ones((8, stream.shape[1]), jnp.bfloat16)
    square = lax.dot_general(ones, high, NT, preferred_element_type=jnp.float32) + lax.dot_general(
        ones, low, NT, preferred_element_type=jnp.float32
    )
    return logits, square


def fill_slots(picks, rows, slot_refs):
    gathered = jnp.dot(picks, rows, preferred_element_type=jnp.float32)
    capacity = slot_refs[0].shape[0]
    for k, out in enumerate(slot_refs):
        out[...] = gathered[k * capacity : (k + 1) * capacity].astype(jnp.bfloat16)


def enter_kernel(expert_count, part_count, me_ref, index_ref, routes_ref, tokens_ref, gain_ref, router_ref, *refs):
    picks_ref, stats_ref = refs[:2]
    slot_refs = refs[2:]
    token_count = tokens_ref.shape[0]
    capacity = slot_refs[0].shape[0]
    relative = lax.broadcasted_iota(jnp.int32, (expert_count, token_count), 0) ^ me_ref[0]
    first, second = routes_ref[0:1, :], routes_ref[1:2, :]
    member = ((relative == first) | (relative == second)).astype(jnp.float32)
    before = lax.broadcasted_iota(jnp.int32, (token_count, token_count), 0)
    after = lax.broadcasted_iota(jnp.int32, (token_count, token_count), 1)
    earlier = (before < after).astype(jnp.bfloat16)
    ranks = jnp.dot(member.astype(jnp.bfloat16), earlier, preferred_element_type=jnp.float32)
    position = lax.broadcasted_iota(jnp.int32, (capacity, token_count), 0).astype(jnp.float32)
    pieces = [
        jnp.where(position == ranks[k : k + 1, :], member[k : k + 1, :], 0.0)
        for k in range(expert_count)
    ]
    picks = jnp.concatenate(pieces, axis=0).astype(jnp.bfloat16)
    picks_ref[...] = picks
    tokens = tokens_ref[...]
    fill_slots(picks, tokens, slot_refs)
    logits, square = make_stats(tokens.astype(jnp.float32), gain_ref[0:1, :], router_ref[...])
    stats_ref[...] = jnp.zeros_like(stats_ref)
    stats_ref[0:expert_count, 0:token_count] = logits
    stats_ref[expert_count : expert_count + 8, 0:token_count] = square
    for part in range(part_count):
        own = (index_ref[0] == part).astype(jnp.float32)
        at = expert_count + 8 + part * LAYERS
        stats_ref[at : at + LAYERS, :] = gain_ref[...] * own


def enter(me, index, routes, tokens, gain, router, capacity, part_count):
    token_count, width = tokens.shape
    expert_count = router.shape[0]
    vmem = pl.BlockSpec(memory_space=pltpu.VMEM)
    return pl.pallas_call(
        functools.partial(enter_kernel, expert_count, part_count),
        in_specs=[pl.BlockSpec(memory_space=pltpu.SMEM)] * 2 + [vmem] * 4,
        out_shape=[
            jax.ShapeDtypeStruct((expert_count * capacity, token_count), jnp.bfloat16),
            jax.ShapeDtypeStruct((expert_count + 8 + part_count * LAYERS, width), jnp.float32),
        ]
        + [jax.ShapeDtypeStruct((capacity, width), jnp.bfloat16)] * expert_count,
        compiler_params=pltpu.CompilerParams(vmem_limit_bytes=32 * MIB),
        cost_estimate=SHORT,
        name="enter",
    )(me, index, routes, tokens, gain, router)


def combine_kernel(expert_count, piece_count, full_width, last, me_ref, *refs):
    routes_ref, picks_ref, stats_ref, stream_ref = refs[:4]
    piece_refs = refs[4 : 4 + piece_count]
    rest = refs[4 + piece_count :]
    token_count = stream_ref.shape[0]
    capacity = picks_ref.shape[0] // expert_count
    first, second = routes_ref[0:1, :], routes_ref[1:2, :]
    logits = stats_ref[0:expert_count, :]
    scale = lax.rsqrt(stats_ref[expert_count : expert_count + 1, :] / full_width + 1e-05)
    expert = lax.broadcasted_iota(jnp.int32, (expert_count, token_count), 0)
    first_logit = jnp.sum(jnp.where(expert == first, logits, 0.0), axis=0, keepdims=True)
    second_logit = jnp.sum(jnp.where(expert == second, logits, 0.0), axis=0, keepdims=True)
    first_weight = 1.0 / (1.0 + jnp.exp((second_logit - first_logit) * scale))
    second_weight = 1.0 - first_weight
    relative = expert ^ me_ref[0]
    weight = jnp.where(relative == first, first_weight, 0.0) + jnp.where(
        relative == second, second_weight, 0.0
    )
    picks = picks_ref[...]
    wide_picks = picks.astype(jnp.float32)
    weighted = jnp.concatenate(
        [
            wide_picks[k * capacity : (k + 1) * capacity] * weight[k : k + 1, :]
            for k in range(expert_count)
        ],
        axis=0,
    )
    high = weighted.astype(jnp.bfloat16)
    low = (weighted - high.astype(jnp.float32)).astype(jnp.bfloat16)
    outs = [piece[...] for piece in piece_refs]
    outs = outs[0] if len(outs) == 1 else jnp.concatenate(outs, axis=0)
    added = lax.dot_general(high, outs, TN, preferred_element_type=jnp.float32)
    added = added + lax.dot_general(low, outs, TN, preferred_element_type=jnp.float32)
    stream = stream_ref[...].astype(jnp.float32) + added
    if last:
        rest[0][...] = stream.astype(jnp.bfloat16)
        return
    gain_ref, router_ref, next_ref, next_stats_ref = rest[:4]
    next_ref[...] = stream
    fill_slots(picks, stream.astype(jnp.bfloat16), rest[4:])
    logits, square = make_stats(stream, gain_ref[...], router_ref[...])
    next_stats_ref[0:expert_count, :] = logits
    next_stats_ref[expert_count:, :] = square


def combine(me, routes, picks, stats, stream, pieces, full_width, following):
    token_count, width = stream.shape
    expert_count = stats.shape[0] - 8
    capacity = picks.shape[0] // expert_count
    if capacity % 16:
        pieces = [jnp.concatenate(pieces, axis=0)]
    vmem = pl.BlockSpec(memory_space=pltpu.VMEM)
    operands = [routes, picks, stats, stream, *pieces]
    if following is None:
        out_shape = [jax.ShapeDtypeStruct((token_count, width), jnp.bfloat16)]
    else:
        operands += following
        out_shape = [
            jax.ShapeDtypeStruct((token_count, width), jnp.float32),
            jax.ShapeDtypeStruct(stats.shape, jnp.float32),
        ] + [jax.ShapeDtypeStruct((capacity, width), jnp.bfloat16)] * expert_count
    return pl.pallas_call(
        functools.partial(
            combine_kernel, expert_count, len(pieces), full_width, following is None
        ),
        in_specs=[pl.BlockSpec(memory_space=pltpu.SMEM)] + [vmem] * len(operands),
        out_shape=out_shape,
        compiler_params=pltpu.CompilerParams(vmem_limit_bytes=32 * MIB),
        cost_estimate=SHORT,
        name="combine",
    )(me, *operands)


def ordered(value, *earlier):
    return lax.optimization_barrier((value, earlier))[0]


def gather_parts(parts, bits):
    parts = dict(parts)
    for bit in bits:
        for j in sorted(parts):
            parts[j ^ 1 << bit] = exchange(parts[j], "tensor", 1 << bit)
    return parts


def per_device(
    tokens,
    routes,
    norm_gain,
    router_weight,
    gate_codes,
    gate_scales,
    up_codes,
    up_scales,
    down_codes,
    down_scales,
):
    part_count = lax.axis_size("tensor")
    expert_count = lax.axis_size("expert")
    bits = part_count.bit_length() - 1
    token_count, width = tokens.shape
    full_width = width * part_count
    hidden = gate_codes.shape[3]
    capacity = 3 * token_count // expert_count
    me = lax.axis_index("expert").astype(jnp.int32).reshape(1)
    index = lax.axis_index("tensor").astype(jnp.int32).reshape(1)
    table = jnp.asarray(block_table(), jnp.bfloat16)
    split = jnp.asarray(split_table(hidden), jnp.bfloat16)
    routes_rows = routes.T
    router_rows = jnp.swapaxes(router_weight, 1, 2)

    picks, stats, *slots = enter(
        me, index, routes_rows, tokens, norm_gain, router_rows[0], capacity, part_count
    )
    first_bits, core_bits = list(reversed(range(1, bits))), [0]
    stream = tokens

    def cores_added(outs):
        kept, away = outs
        return [(kept, 1), (exchange(away, "tensor", 1), 1)]

    def leaving_of(terms):
        total = sum(array[step :: 2 * step].astype(jnp.float32) for array, step in terms)
        return total.astype(jnp.bfloat16)

    def rest_added(terms, leaving):
        for bit in range(1, bits):
            if bit > 1:
                leaving = leaving_of(terms)
            terms = [(array, 2 * step) for array, step in terms]
            terms.append((exchange(leaving, "tensor", 1 << bit), 1))
        return [array for array, _ in terms]

    def give_back(terms, chunk, returned):
        pieces = add_split(terms, capacity)
        for k, piece in zip(chunk, pieces):
            returned[k] = piece if k == 0 else exchange(piece, "expert", k)
        return pieces

    unit = max(1, expert_count // 8)
    groups = {
        name: [k for u in units for k in range(u * unit, (u + 1) * unit)]
        for name, units in GROUPS
    }
    prepared = {}
    gains = None
    for layer_idx in range(LAYERS):
        arrived = {0: slots[0]}

        def sent(name, slots=slots):
            for k in groups[name]:
                if k not in arrived:
                    arrived[k] = exchange(slots[k], "expert", k)
            return [arrived[k] for k in groups[name]]

        returned = [None] * expert_count
        rows, parts, outs, terms = {}, {}, {}, {}
        token = None
        for step, chained in ORDERS[layer_idx]:
            kind, name = step[0], step[1:]

            def wait(value):
                if not chained or token is None:
                    return value
                return ordered(value, token)

            if kind == "R":
                if name not in rows:
                    rows[name] = jnp.concatenate(wait(sent(name)), axis=0)
                else:
                    rows[name] = wait(rows[name])
                parts[name] = gather_parts({0: rows[name]}, first_bits)
                token = rows[name]
            elif kind == "C":
                held = dict(wait(parts[name]))
                token = [held[j] for j in sorted(held) if j > 0]
                held[0] = ordered(held[0], token)
                parts[name] = gather_parts(held, core_bits)
            elif kind == "E":
                outs[name] = expert_parts(
                    layer_idx,
                    wait(index),
                    [parts[name][j] for j in range(part_count)],
                    gains,
                    *[prepared[w, layer_idx] for w in "gud"],
                    split,
                )
                token = outs[name]
                terms[name] = cores_added(outs[name])
            elif kind == "X":
                leaving = wait(leaving_of(terms[name]))
                terms[name] = rest_added(terms[name], leaving)
                token = leaving
            elif kind == "P":
                token = give_back(wait(terms[name]), groups[name], returned)
            elif kind == "Z":
                sent(name, wait(slots))
            elif kind == "N":
                rows[name] = jnp.concatenate(wait(sent(name)), axis=0)
                token = rows[name]
            elif kind == "W":
                at = int(name[1:])
                if name[0] == "d":
                    prepared["d", at] = out_weights(down_codes, wait(down_scales), at)
                else:
                    codes, scales = {"g": (gate_codes, gate_scales), "u": (up_codes, up_scales)}[name[0]]
                    prepared[name[0], at] = in_weights(codes, scales, wait(table), at)
                token = prepared[name[0], at]
            elif kind == "S":
                stats = wait(stats)
                for bit in range(bits):
                    stats = stats + exchange(stats, "tensor", 1 << bit)
                if layer_idx == 0:
                    gains = stats[expert_count + 8 :]
                    stats = stats[: expert_count + 8, :token_count]
                token = stats
            elif kind == "T":
                token = stats
        following = None
        if layer_idx + 1 < LAYERS:
            following = [norm_gain[layer_idx + 1 : layer_idx + 2], router_rows[layer_idx + 1]]
            ready = [value for (_, at), value in prepared.items() if at > layer_idx]
            if ready:
                me = ordered(me, ready)
        results = combine(
            me, routes_rows, picks, stats, stream, returned, full_width, following
        )
        if following is None:
            return results[0]
        stream, stats, *slots = results


def solution(mesh):
    in_specs = (
        P("expert", "tensor"),
        P("expert", None),
        P(None, "tensor"),
        P(None, "tensor", None),
        P(None, "expert", None, "tensor"),
        P(None, "expert", None, "tensor"),
        P(None, "expert", None, "tensor"),
        P(None, "expert", None, "tensor"),
        P(None, "expert", "tensor", None),
        P(None, "expert", "tensor", None),
    )
    out_specs = P("expert", "tensor")
    return jax.shard_map(
        per_device, mesh=mesh, in_specs=in_specs, out_specs=out_specs, check_vma=False
    )
```

```python
import functools
import math

import jax
import jax.numpy as jnp
import numpy as np
from jax import lax
from jax.experimental import pallas as pl
from jax.experimental.pallas import tpu as pltpu
from jax.sharding import PartitionSpec as P

LAYERS = 2
ORDERS = (
    (
        ("S", 0), ("Ra", 1), ("Wg0", 1), ("Wd0", 1), ("Wu0", 1), ("Rb", 1), ("Ca", 0),
        ("Ea", 0), ("Cb", 1), ("Xa", 0), ("Eb", 0), ("Xb", 1), ("Wg1", 1), ("Pb", 1),
        ("Wu1", 1), ("Pa", 1), ("Wd1", 1),
    ),
    (
        ("S", 1), ("Ra", 0), ("Rb", 0), ("Ca", 1), ("Ea", 1), ("Cb", 1), ("Eb", 1), ("Xb", 1),
        ("Xa", 0), ("Pb", 1), ("Pa", 1),
    ),
)
GROUPS = (
    ("a", (0, 1, 2, 3)),
    ("b", (4, 5, 6, 7)),
)
GROUP = 128
BLOCK = 256
MIB = 1 << 20
FIRST = 8
SECOND = 64
NT = (((1,), (1,)), ((), ()))
TN = (((0,), (0,)), ((), ()))


def exchange(shard, axis, mask):
    return lax.ppermute(shard, axis, [(i, i ^ mask) for i in range(lax.axis_size(axis))])


def block_table():
    index = np.arange(BLOCK)
    order = np.concatenate([index[0::2], index[1::2]])
    common = index[:, None] & order[None, :]
    ones = np.array([bin(v).count("1") for v in range(BLOCK)])[common]
    return np.where(ones % 2 == 1, -1.0, 1.0).astype(np.float32)


def split_table(width):
    table = np.zeros((width, width), np.float32)
    for unit in range(width):
        table[unit, unit % 2 * (width // 2) + unit // 2] = 1.0
    return table


def power(exponents):
    return (1 << (16 - exponents)).astype(jnp.float32) * (1.0 / 65536.0)


SHORT = pl.CostEstimate(flops=1000, bytes_accessed=1000, transcendentals=0)


def butterfly(rows, start):
    stride = start
    while stride < len(rows):
        for b in range(len(rows)):
            if b & stride == 0:
                low, high = rows[b], rows[b + stride]
                rows[b], rows[b + stride] = low + high, low - high
        stride *= 2


def in_weights_kernel(first_steps, words_ref, scales_ref, table_ref, out_ref, sums_ref):
    half = BLOCK // 2
    words_group = GROUP // 2
    groups_block = BLOCK // GROUP
    step = pl.program_id(0)
    width = words_ref.shape[3]
    block_count = out_ref.shape[0]

    @pl.when(step < first_steps)
    def _():
        sums = []
        for q in range(FIRST):
            words = words_ref[0, 0, q * half : (q + 1) * half, :]
            pieces = []
            for shift in (0, 4):
                codes = ((words >> shift) & 15).astype(jnp.float32) - 8.0
                for g in range(groups_block):
                    at = q * groups_block + g
                    factor = power(scales_ref[0, 0, at : at + 1, :])
                    pieces.append(codes[g * words_group : (g + 1) * words_group] * factor)
            block = jnp.concatenate(pieces, axis=0).astype(jnp.bfloat16)
            sums.append(jnp.dot(table_ref[...], block, preferred_element_type=jnp.float32))
        butterfly(sums, 1)
        for q in range(FIRST):
            sums_ref[step * FIRST + q] = sums[q]

    @pl.when(step >= first_steps)
    def _():
        base = (step - first_steps) * SECOND
        for r in range(0, SECOND, 16):
            for c in range(0, width, 128):
                for q in range(FIRST):
                    rows = [
                        sums_ref[b * FIRST + q, pl.ds(pl.multiple_of(base + r, 16), 16), c : c + 128]
                        for b in range(block_count // FIRST)
                    ]
                    butterfly(rows, 1)
                    for b, row in enumerate(rows):
                        out_ref[b * FIRST + q, r : r + 16, c : c + 128] = row.astype(jnp.bfloat16)


def in_weights(words, scales, table, layer_idx):
    _, _, word_rows, width = words.shape
    full = 2 * word_rows
    block_count = full // BLOCK
    first_steps = block_count // FIRST
    word_tile = FIRST * BLOCK // 2
    group_tile = FIRST * BLOCK // GROUP
    out = pl.pallas_call(
        functools.partial(in_weights_kernel, first_steps),
        grid=(first_steps + BLOCK // SECOND,),
        in_specs=[
            pl.BlockSpec(
                (1, 1, word_tile, width),
                lambda i: (layer_idx, 0, jnp.minimum(i, first_steps - 1), 0),
            ),
            pl.BlockSpec(
                (1, 1, group_tile, width),
                lambda i: (layer_idx, 0, jnp.minimum(i, first_steps - 1), 0),
            ),
            pl.BlockSpec((BLOCK, BLOCK), lambda i: (0, 0)),
        ],
        out_specs=pl.BlockSpec(
            (block_count, SECOND, width), lambda i: (0, jnp.maximum(i - first_steps, 0), 0)
        ),
        out_shape=jax.ShapeDtypeStruct((block_count, BLOCK, width), jnp.bfloat16),
        scratch_shapes=[pltpu.VMEM((block_count, BLOCK, width), jnp.float32)],
        compiler_params=pltpu.CompilerParams(vmem_limit_bytes=54 * MIB),
        cost_estimate=SHORT,
        name="in_weights",
    )(words, scales, table)
    return out.reshape(full, width)


def out_weights_kernel(words_ref, scales_ref, out_ref):
    words = words_ref[0, 0]
    word_rows = words.shape[0]
    words_group = GROUP // 2
    for part, shift in enumerate((0, 4)):
        codes = ((words >> shift) & 15).astype(jnp.float32) - 8.0
        for g in range(word_rows // words_group):
            factor = power(scales_ref[0, 0, pl.ds(g, 1), :])
            out_ref[pl.ds(part * word_rows + g * words_group, words_group), :] = (
                codes[g * words_group : (g + 1) * words_group] * factor
            ).astype(jnp.bfloat16)


def out_weights(words, scales, layer_idx):
    _, _, word_rows, width = words.shape
    groups = scales.shape[2]
    tile = width // 2
    return pl.pallas_call(
        out_weights_kernel,
        grid=(width // tile,),
        in_specs=[
            pl.BlockSpec((1, 1, word_rows, tile), lambda c: (layer_idx, 0, 0, c)),
            pl.BlockSpec((1, 1, groups, tile), lambda c: (layer_idx, 0, 0, c)),
        ],
        out_specs=pl.BlockSpec((2 * word_rows, tile), lambda c: (0, c)),
        out_shape=jax.ShapeDtypeStruct((2 * word_rows, width), jnp.bfloat16),
        compiler_params=pltpu.CompilerParams(vmem_limit_bytes=54 * MIB),
        cost_estimate=SHORT,
        name="out_weights",
    )(words, scales)


def expert_kernel(part_count, full_width, layer_idx, index_ref, *refs):
    x_refs, refs = refs[:part_count], refs[part_count:]
    gains_ref, split_ref, gate_ref, up_ref, down_ref = refs[:5]
    refs = refs[1:]
    out_refs, refs = refs[4:6], refs[6:]
    width = x_refs[0].shape[1]
    gate = up = square = None
    for j in range(part_count):
        wide = x_refs[j][...].astype(jnp.float32)
        gain = gains_ref[pl.ds((index_ref[0] ^ j) * LAYERS + layer_idx, 1), :]
        rows = (wide * gain).astype(jnp.bfloat16)
        part = jnp.sum(wide * wide, axis=1, keepdims=True)
        square = part if j == 0 else square + part
        at = pl.ds(pl.multiple_of((index_ref[0] ^ j) * width, width), width)
        part = jnp.dot(rows, gate_ref[at, :], preferred_element_type=jnp.float32)
        gate = part if j == 0 else gate + part
        part = jnp.dot(rows, up_ref[at, :], preferred_element_type=jnp.float32)
        up = part if j == 0 else up + part
    scale = lax.rsqrt(square / full_width + 1e-05) * (1.0 / math.sqrt(full_width))
    gate = gate * scale
    act = (gate / (1.0 + jnp.exp(-gate))) * (up * scale)
    act = jnp.dot(
        act.astype(jnp.bfloat16), split_ref[...], preferred_element_type=jnp.float32
    ).astype(jnp.bfloat16)
    for j in range(part_count):
        at = pl.ds(pl.multiple_of((index_ref[0] ^ j) * width, width), width)
        out_refs[j % 2][j // 2] = jnp.dot(
            act, down_ref[:, at], preferred_element_type=jnp.float32
        ).astype(jnp.bfloat16)


def expert_parts(layer_idx, index, parts, gains, gate_w, up_w, down_w, split):
    part_count = len(parts)
    row_count, width = parts[0].shape
    full_width, hidden = gate_w.shape
    vmem = pl.BlockSpec(memory_space=pltpu.VMEM)
    return pl.pallas_call(
        functools.partial(expert_kernel, part_count, full_width, layer_idx),
        in_specs=[pl.BlockSpec(memory_space=pltpu.SMEM)]
        + [vmem] * (part_count + 5),
        out_specs=[vmem] * 2,
        out_shape=[jax.ShapeDtypeStruct((part_count // 2, row_count, width), jnp.bfloat16)] * 2,
        compiler_params=pltpu.CompilerParams(vmem_limit_bytes=16 * MIB),
        cost_estimate=SHORT,
        name="expert_parts",
    )(index, *parts, gains, split, gate_w, up_w, down_w)


def add_split_kernel(term_count, *refs):
    total = refs[0][0].astype(jnp.float32)
    for term in refs[1:term_count]:
        total = total + term[0].astype(jnp.float32)
    at = 0
    for out in refs[term_count:]:
        rows = out.shape[0]
        out[...] = total[at : at + rows].astype(jnp.bfloat16)
        at += rows


def add_split(terms, piece_rows):
    _, row_count, width = terms[0].shape
    vmem = pl.BlockSpec(memory_space=pltpu.VMEM)
    count = row_count // piece_rows
    return pl.pallas_call(
        functools.partial(add_split_kernel, len(terms)),
        in_specs=[vmem] * len(terms),
        out_specs=[vmem] * count,
        out_shape=[jax.ShapeDtypeStruct((piece_rows, width), jnp.bfloat16)] * count,
        compiler_params=pltpu.CompilerParams(vmem_limit_bytes=32 * MIB),
        cost_estimate=SHORT,
        name="add_split",
    )(*terms)


def make_stats(stream, gain, router):
    scaled = (stream * gain).astype(jnp.bfloat16)
    logits = lax.dot_general(router, scaled, NT, preferred_element_type=jnp.float32)
    squares = stream * stream
    high = squares.astype(jnp.bfloat16)
    low = (squares - high.astype(jnp.float32)).astype(jnp.bfloat16)
    ones = jnp.ones((8, stream.shape[1]), jnp.bfloat16)
    square = lax.dot_general(ones, high, NT, preferred_element_type=jnp.float32) + lax.dot_general(
        ones, low, NT, preferred_element_type=jnp.float32
    )
    return logits, square


def fill_slots(picks, rows, slot_refs):
    gathered = jnp.dot(picks, rows, preferred_element_type=jnp.float32)
    capacity = slot_refs[0].shape[0]
    for k, out in enumerate(slot_refs):
        out[...] = gathered[k * capacity : (k + 1) * capacity].astype(jnp.bfloat16)


def enter_kernel(expert_count, part_count, me_ref, index_ref, routes_ref, tokens_ref, gain_ref, router_ref, *refs):
    picks_ref, stats_ref = refs[:2]
    slot_refs = refs[2:]
    token_count = tokens_ref.shape[0]
    capacity = slot_refs[0].shape[0]
    relative = lax.broadcasted_iota(jnp.int32, (expert_count, token_count), 0) ^ me_ref[0]
    first, second = routes_ref[0:1, :], routes_ref[1:2, :]
    member = ((relative == first) | (relative == second)).astype(jnp.float32)
    before = lax.broadcasted_iota(jnp.int32, (token_count, token_count), 0)
    after = lax.broadcasted_iota(jnp.int32, (token_count, token_count), 1)
    earlier = (before < after).astype(jnp.bfloat16)
    ranks = jnp.dot(member.astype(jnp.bfloat16), earlier, preferred_element_type=jnp.float32)
    position = lax.broadcasted_iota(jnp.int32, (capacity, token_count), 0).astype(jnp.float32)
    pieces = [
        jnp.where(position == ranks[k : k + 1, :], member[k : k + 1, :], 0.0)
        for k in range(expert_count)
    ]
    picks = jnp.concatenate(pieces, axis=0).astype(jnp.bfloat16)
    picks_ref[...] = picks
    tokens = tokens_ref[...]
    fill_slots(picks, tokens, slot_refs)
    logits, square = make_stats(tokens.astype(jnp.float32), gain_ref[0:1, :], router_ref[...])
    stats_ref[...] = jnp.zeros_like(stats_ref)
    stats_ref[0:expert_count, 0:token_count] = logits
    stats_ref[expert_count : expert_count + 8, 0:token_count] = square
    for part in range(part_count):
        own = (index_ref[0] == part).astype(jnp.float32)
        at = expert_count + 8 + part * LAYERS
        stats_ref[at : at + LAYERS, :] = gain_ref[...] * own


def enter(me, index, routes, tokens, gain, router, capacity, part_count):
    token_count, width = tokens.shape
    expert_count = router.shape[0]
    vmem = pl.BlockSpec(memory_space=pltpu.VMEM)
    return pl.pallas_call(
        functools.partial(enter_kernel, expert_count, part_count),
        in_specs=[pl.BlockSpec(memory_space=pltpu.SMEM)] * 2 + [vmem] * 4,
        out_shape=[
            jax.ShapeDtypeStruct((expert_count * capacity, token_count), jnp.bfloat16),
            jax.ShapeDtypeStruct((expert_count + 8 + part_count * LAYERS, width), jnp.float32),
        ]
        + [jax.ShapeDtypeStruct((capacity, width), jnp.bfloat16)] * expert_count,
        compiler_params=pltpu.CompilerParams(vmem_limit_bytes=32 * MIB),
        cost_estimate=SHORT,
        name="enter",
    )(me, index, routes, tokens, gain, router)


def combine_kernel(expert_count, piece_count, full_width, last, me_ref, *refs):
    routes_ref, picks_ref, stats_ref, stream_ref = refs[:4]
    piece_refs = refs[4 : 4 + piece_count]
    rest = refs[4 + piece_count :]
    token_count = stream_ref.shape[0]
    capacity = picks_ref.shape[0] // expert_count
    first, second = routes_ref[0:1, :], routes_ref[1:2, :]
    logits = stats_ref[0:expert_count, :]
    scale = lax.rsqrt(stats_ref[expert_count : expert_count + 1, :] / full_width + 1e-05)
    expert = lax.broadcasted_iota(jnp.int32, (expert_count, token_count), 0)
    first_logit = jnp.sum(jnp.where(expert == first, logits, 0.0), axis=0, keepdims=True)
    second_logit = jnp.sum(jnp.where(expert == second, logits, 0.0), axis=0, keepdims=True)
    first_weight = 1.0 / (1.0 + jnp.exp((second_logit - first_logit) * scale))
    second_weight = 1.0 - first_weight
    relative = expert ^ me_ref[0]
    weight = jnp.where(relative == first, first_weight, 0.0) + jnp.where(
        relative == second, second_weight, 0.0
    )
    picks = picks_ref[...]
    wide_picks = picks.astype(jnp.float32)
    weighted = jnp.concatenate(
        [
            wide_picks[k * capacity : (k + 1) * capacity] * weight[k : k + 1, :]
            for k in range(expert_count)
        ],
        axis=0,
    )
    high = weighted.astype(jnp.bfloat16)
    low = (weighted - high.astype(jnp.float32)).astype(jnp.bfloat16)
    outs = [piece[...] for piece in piece_refs]
    outs = outs[0] if len(outs) == 1 else jnp.concatenate(outs, axis=0)
    added = lax.dot_general(high, outs, TN, preferred_element_type=jnp.float32)
    added = added + lax.dot_general(low, outs, TN, preferred_element_type=jnp.float32)
    stream = stream_ref[...].astype(jnp.float32) + added
    if last:
        rest[0][...] = stream.astype(jnp.bfloat16)
        return
    gain_ref, router_ref, next_ref, next_stats_ref = rest[:4]
    next_ref[...] = stream
    fill_slots(picks, stream.astype(jnp.bfloat16), rest[4:])
    logits, square = make_stats(stream, gain_ref[...], router_ref[...])
    next_stats_ref[0:expert_count, :] = logits
    next_stats_ref[expert_count:, :] = square


def combine(me, routes, picks, stats, stream, pieces, full_width, following):
    token_count, width = stream.shape
    expert_count = stats.shape[0] - 8
    capacity = picks.shape[0] // expert_count
    if capacity % 16:
        pieces = [jnp.concatenate(pieces, axis=0)]
    vmem = pl.BlockSpec(memory_space=pltpu.VMEM)
    operands = [routes, picks, stats, stream, *pieces]
    if following is None:
        out_shape = [jax.ShapeDtypeStruct((token_count, width), jnp.bfloat16)]
    else:
        operands += following
        out_shape = [
            jax.ShapeDtypeStruct((token_count, width), jnp.float32),
            jax.ShapeDtypeStruct(stats.shape, jnp.float32),
        ] + [jax.ShapeDtypeStruct((capacity, width), jnp.bfloat16)] * expert_count
    return pl.pallas_call(
        functools.partial(
            combine_kernel, expert_count, len(pieces), full_width, following is None
        ),
        in_specs=[pl.BlockSpec(memory_space=pltpu.SMEM)] + [vmem] * len(operands),
        out_shape=out_shape,
        compiler_params=pltpu.CompilerParams(vmem_limit_bytes=32 * MIB),
        cost_estimate=SHORT,
        name="combine",
    )(me, *operands)


def ordered(value, *earlier):
    return lax.optimization_barrier((value, earlier))[0]


def gather_parts(parts, bits):
    parts = dict(parts)
    for bit in bits:
        for j in sorted(parts):
            parts[j ^ 1 << bit] = exchange(parts[j], "tensor", 1 << bit)
    return parts


def per_device(
    tokens,
    routes,
    norm_gain,
    router_weight,
    gate_codes,
    gate_scales,
    up_codes,
    up_scales,
    down_codes,
    down_scales,
):
    part_count = lax.axis_size("tensor")
    expert_count = lax.axis_size("expert")
    bits = part_count.bit_length() - 1
    token_count, width = tokens.shape
    full_width = width * part_count
    hidden = gate_codes.shape[3]
    capacity = 3 * token_count // expert_count
    me = lax.axis_index("expert").astype(jnp.int32).reshape(1)
    index = lax.axis_index("tensor").astype(jnp.int32).reshape(1)
    table = jnp.asarray(block_table(), jnp.bfloat16)
    split = jnp.asarray(split_table(hidden), jnp.bfloat16)
    routes_rows = routes.T
    router_rows = jnp.swapaxes(router_weight, 1, 2)

    picks, stats, *slots = enter(
        me, index, routes_rows, tokens, norm_gain, router_rows[0], capacity, part_count
    )
    first_bits, core_bits = list(reversed(range(1, bits))), [0]
    stream = tokens

    def cores_added(outs):
        kept, away = outs
        return [(kept, 1), (exchange(away, "tensor", 1), 1)]

    def leaving_of(terms):
        total = sum(array[step :: 2 * step].astype(jnp.float32) for array, step in terms)
        return total.astype(jnp.bfloat16)

    def rest_added(terms, leaving):
        for bit in range(1, bits):
            if bit > 1:
                leaving = leaving_of(terms)
            terms = [(array, 2 * step) for array, step in terms]
            terms.append((exchange(leaving, "tensor", 1 << bit), 1))
        return [array for array, _ in terms]

    def give_back(terms, chunk, returned):
        pieces = add_split(terms, capacity)
        for k, piece in zip(chunk, pieces):
            returned[k] = piece if k == 0 else exchange(piece, "expert", k)
        return pieces

    unit = max(1, expert_count // 8)
    groups = {
        name: [k for u in units for k in range(u * unit, (u + 1) * unit)]
        for name, units in GROUPS
    }
    prepared = {}
    gains = None
    for layer_idx in range(LAYERS):
        arrived = {0: slots[0]}

        def sent(name, slots=slots):
            for k in groups[name]:
                if k not in arrived:
                    arrived[k] = exchange(slots[k], "expert", k)
            return [arrived[k] for k in groups[name]]

        returned = [None] * expert_count
        rows, parts, outs, terms = {}, {}, {}, {}
        token = None
        for step, chained in ORDERS[layer_idx]:
            kind, name = step[0], step[1:]

            def wait(value):
                if not chained or token is None:
                    return value
                return ordered(value, token)

            if kind == "R":
                if name not in rows:
                    rows[name] = jnp.concatenate(wait(sent(name)), axis=0)
                else:
                    rows[name] = wait(rows[name])
                parts[name] = gather_parts({0: rows[name]}, first_bits)
                token = rows[name]
            elif kind == "C":
                held = dict(wait(parts[name]))
                token = [held[j] for j in sorted(held) if j > 0]
                held[0] = ordered(held[0], token)
                parts[name] = gather_parts(held, core_bits)
            elif kind == "E":
                outs[name] = expert_parts(
                    layer_idx,
                    wait(index),
                    [parts[name][j] for j in range(part_count)],
                    gains,
                    *[prepared[w, layer_idx] for w in "gud"],
                    split,
                )
                token = outs[name]
                terms[name] = cores_added(outs[name])
            elif kind == "X":
                leaving = wait(leaving_of(terms[name]))
                terms[name] = rest_added(terms[name], leaving)
                token = leaving
            elif kind == "P":
                token = give_back(wait(terms[name]), groups[name], returned)
            elif kind == "Z":
                sent(name, wait(slots))
            elif kind == "N":
                rows[name] = jnp.concatenate(wait(sent(name)), axis=0)
                token = rows[name]
            elif kind == "W":
                at = int(name[1:])
                if name[0] == "d":
                    prepared["d", at] = out_weights(down_codes, wait(down_scales), at)
                else:
                    codes, scales = {"g": (gate_codes, gate_scales), "u": (up_codes, up_scales)}[name[0]]
                    prepared[name[0], at] = in_weights(codes, scales, wait(table), at)
                token = prepared[name[0], at]
            elif kind == "S":
                stats = wait(stats)
                for bit in range(bits):
                    stats = stats + exchange(stats, "tensor", 1 << bit)
                if layer_idx == 0:
                    gains = stats[expert_count + 8 :]
                    stats = stats[: expert_count + 8, :token_count]
                token = stats
            elif kind == "T":
                token = stats
        following = None
        if layer_idx + 1 < LAYERS:
            following = [norm_gain[layer_idx + 1 : layer_idx + 2], router_rows[layer_idx + 1]]
            ready = [value for (_, at), value in prepared.items() if at > layer_idx]
            if ready:
                me = ordered(me, ready)
        results = combine(
            me, routes_rows, picks, stats, stream, returned, full_width, following
        )
        if following is None:
            return results[0]
        stream, stats, *slots = results


def solution(mesh):
    in_specs = (
        P("expert", "tensor"),
        P("expert", None),
        P(None, "tensor"),
        P(None, "tensor", None),
        P(None, "expert", None, "tensor"),
        P(None, "expert", None, "tensor"),
        P(None, "expert", None, "tensor"),
        P(None, "expert", None, "tensor"),
        P(None, "expert", "tensor", None),
        P(None, "expert", "tensor", None),
    )
    out_specs = P("expert", "tensor")
    return jax.shard_map(
        per_device, mesh=mesh, in_specs=in_specs, out_specs=out_specs, check_vma=False
    )
```
